32 devices in a mesh: cp: 8 (over z, x), dp: 4 (over y, core).
Axes of the slice: x: 2, y: 2, z: 4, core: 2. Of those that a mesh axis runs over, the one named last changes fastest.
Arguments:
- queries: bfloat16 [4, 1024, 2560], P('dp', 'cp'), may hold values from -6 to 6
- keys: bfloat16 [4, 1024, 2560], P('dp', 'cp'), may hold values from -6 to 6
- values: bfloat16 [4, 1024, 2560], P('dp', 'cp'), may hold values from -6 to 6
- outputs: bfloat16 [4, 1024, 2560], P('dp', 'cp'), may hold values from -6 to 6
- d_out: bfloat16 [4, 1024, 2560], P('dp', 'cp'), may hold values from -6 to 6
- log_norm: float32 [4, 1024, 20], P('dp', 'cp'), may hold values from 3 to 7
- lengths: int32 [4, 3], P('dp'), may hold values from 1 to 4, as said below
- fire_w1: float32 [32], replicated, may hold values from -6 to 6
- fire_b1: float32 [32], replicated, may hold values from -3 to 3
- fire_w2: float32 [32, 20], replicated, may hold values from -1 to 1
Outputs:
- grad_queries: bfloat16 [4, 1024, 2560], P('dp', 'cp')
- grad_keys: bfloat16 [4, 1024, 2560], P('dp', 'cp')
- grad_values: bfloat16 [4, 1024, 2560], P('dp', 'cp')
- grad_w1: float32 [32], replicated
- grad_b1: float32 [32], replicated
- grad_w2: float32 [32, 20], replicated
The draws below stay inside these ranges and needn't reach their ends.
Inputs may be any that keep to these rules, and one draw needn't show every extreme that they name: `lengths`: each batch row's 3 sequences fill its 8 blocks in order, each a whole number of blocks; the first sequence of every row takes exactly 4 blocks.
All inputs are finite; a program needn't handle non-finite values.
Results may differ from the reference program's by a relative error of at most 0.0054.
Values may be sent and summed in bfloat16 or wider, within the bound.
A program may use at most 128 MiB of HBM per device.

```python
import jax
import jax.numpy as jnp
from jax import lax

HEADS = 20
HEAD_DIM = 128
FIRE_HID = 32
TOK_DEV = 128
GROUP_MOST = 4
WIDTH = 2560
TOKENS = 1024
NSEQ = 3
N_CP = 8
N_DP = 4


def draw_lengths(key, part):
    slots = NSEQ - 1
    spare = GROUP_MOST - 1
    units = slots * spare
    extra = N_CP - GROUP_MOST - slots
    row_keys = jax.random.split(jax.random.fold_in(key, 17), N_DP)

    def one_row(row_key):
        order = jax.random.permutation(row_key, units)
        chosen = (order < extra).astype(jnp.int32)
        owner = jnp.arange(units, dtype=jnp.int32) // spare
        counts = jnp.sum((owner[None, :] == jnp.arange(slots, dtype=jnp.int32)[:, None]).astype(jnp.int32) * chosen[None, :], axis=1)
        return jnp.concatenate([jnp.full((1,), GROUP_MOST, jnp.int32), (1 + counts).astype(jnp.int32)])
    return jax.vmap(one_row)(row_keys).astype(jnp.int32)


def block_scale(rng, extent, cuts, least, top_value):
    level, own = 1.0, jax.random.fold_in(rng, 6)
    for position, parts in cuts:
        steps = jnp.exp(jax.random.uniform(jax.random.fold_in(own, position), (parts,), jnp.float32, least / len(cuts), top_value / len(cuts)))
        level = level * jnp.repeat(steps, extent[position] // parts).reshape([-1 if axis == position else 1 for axis in range(len(extent))])
    return level


def normal_values(own_key, dims, width, limit, cuts=(), held_as=jnp.bfloat16):
    loudness = block_scale(own_key, dims, cuts, -0.22, 0.18) if cuts else 1.0
    values = jax.random.normal(own_key, dims, jnp.float32) * width * loudness
    return jnp.minimum(jnp.maximum(values, -limit), limit).astype(held_as)


def setup_inputs(seed: int = 0) -> dict:
    key_list = jax.random.split(jax.random.key(seed), 11)
    queries = normal_values(key_list[0], (N_DP, TOKENS, WIDTH), 1.0, 6.0, ((0, 4), (1, 8)))
    keys = normal_values(key_list[1], (N_DP, TOKENS, WIDTH), 1.0, 6.0, ((0, 4), (1, 8)))
    values = normal_values(key_list[2], (N_DP, TOKENS, WIDTH), 1.0, 6.0, ((0, 4), (1, 8)))
    outputs = normal_values(key_list[3], (N_DP, TOKENS, WIDTH), 1.0, 6.0, ((0, 4), (1, 8)))
    d_out = normal_values(key_list[4], (N_DP, TOKENS, WIDTH), 1.0, 6.0, ((0, 4), (1, 8)))
    log_norm = jnp.clip(3.0 + 4.0 * jax.random.uniform(key_list[5], (N_DP, TOKENS, HEADS), jnp.float32) ** block_scale(key_list[5], (N_DP, TOKENS, HEADS), ((0, 4), (1, 8)), -0.2, 0.2), 3.0, 7.0)
    lengths = draw_lengths(jax.random.fold_in(key_list[10], 71), 0)
    fire_w1 = normal_values(key_list[7], (FIRE_HID,), 2.0, 6.0, (), jnp.float32)
    fire_b1 = normal_values(key_list[8], (FIRE_HID,), 0.5, 3.0, (), jnp.float32)
    fire_w2 = normal_values(key_list[9], (FIRE_HID, HEADS), FIRE_HID ** -0.5, 1.0, (), jnp.float32)
    return {"queries": queries, "keys": keys, "values": values, "outputs": outputs, "d_out": d_out, "log_norm": log_norm, "lengths": lengths, "fire_w1": fire_w1, "fire_b1": fire_b1, "fire_w2": fire_w2}


fire_floor = 64.0


def seat_of(length_row, device):
    ends = jnp.cumsum(length_row)
    sequence = jnp.sum((ends <= device).astype(jnp.int32))
    before = jnp.sum(jnp.where(jnp.arange(length_row.shape[0], dtype=jnp.int32) < sequence, length_row, 0))
    return sequence, device - before


def pair_terms(query_heads, grad_heads, log_block, delta_block, key_heads, value_heads, query_seq, query_pos, key_seq, key_pos, fire_w1, fire_b1, fire_w2):
    highest = lax.Precision.HIGHEST
    scale_value = query_heads.shape[2] ** -0.5
    allowed = (query_seq == key_seq) & (key_pos[None, :] <= query_pos[:, None])
    distance = jnp.maximum(query_pos[:, None] - key_pos[None, :], 0).astype(jnp.float32)
    denom = jnp.log1p(jnp.maximum(query_pos.astype(jnp.float32), fire_floor))
    ratio = jnp.log1p(distance) / denom[:, None]
    hidden_pre = fire_w1[:, None, None] * ratio[None] + fire_b1[:, None, None]
    hidden_act = jnp.maximum(hidden_pre, 0.0)
    pair_bias = jnp.einsum("cqk,ch->hqk", hidden_act, fire_w2, precision=highest)
    query_f = query_heads.astype(jnp.float32)
    key_f = key_heads.astype(jnp.float32)
    value_f = value_heads.astype(jnp.float32)
    grad_f = grad_heads.astype(jnp.float32)
    scores = jnp.einsum("qhd,khd->hqk", query_f, key_f) * scale_value + pair_bias
    shifted = jnp.where(allowed[None], scores - log_block.T[:, :, None], -1e30)
    prob_block = jnp.exp(shifted)
    dprob = jnp.einsum("qhd,khd->hqk", grad_f, value_f)
    dscore = prob_block * (dprob - delta_block.T[:, :, None])
    prob_low = lax.optimization_barrier(prob_block.astype(jnp.bfloat16)).astype(jnp.float32)
    score_low = lax.optimization_barrier(dscore.astype(jnp.bfloat16)).astype(jnp.float32)
    grad_query = jnp.einsum("hqk,khd->qhd", score_low, key_f) * scale_value
    grad_key = jnp.einsum("hqk,qhd->khd", score_low, query_f) * scale_value
    grad_value = jnp.einsum("hqk,qhd->khd", prob_low, grad_f)
    grad_second = jnp.einsum("hqk,cqk->ch", dscore, hidden_act, precision=highest)
    grad_act = jnp.einsum("hqk,ch->cqk", dscore, fire_w2, precision=highest)
    grad_pre = jnp.where(hidden_pre > 0, grad_act, 0.0)
    grad_first = jnp.sum(grad_pre * ratio[None], axis=(1, 2))
    grad_bias = jnp.sum(grad_pre, axis=(1, 2))
    return grad_query, grad_key, grad_value, grad_first, grad_bias, grad_second


def reference(queries, keys, values, outputs, d_out, log_norm, lengths, fire_w1, fire_b1, fire_w2):
    block_shape = (N_CP, TOK_DEV, HEADS, HEAD_DIM)
    total_first = jnp.zeros((FIRE_HID,), jnp.float32)
    total_bias = jnp.zeros((FIRE_HID,), jnp.float32)
    total_second = jnp.zeros((FIRE_HID, HEADS), jnp.float32)
    all_q, all_k, all_v = [], [], []
    for batch_row in range(N_DP):
        query_blocks = queries[batch_row].reshape(block_shape)
        key_blocks = keys[batch_row].reshape(block_shape)
        value_blocks = values[batch_row].reshape(block_shape)
        grad_blocks = d_out[batch_row].reshape(block_shape)
        out_blocks = outputs[batch_row].reshape(block_shape)
        log_blocks = log_norm[batch_row].reshape(N_CP, TOK_DEV, HEADS)
        delta_blocks = jnp.einsum("nqhd,nqhd->nqh", grad_blocks.astype(jnp.float32), out_blocks.astype(jnp.float32))
        length_row = lengths[batch_row]
        seq_ids, offsets = jax.vmap(lambda device: seat_of(length_row, device))(jnp.arange(N_CP, dtype=jnp.int32))
        positions = offsets[:, None] * TOK_DEV + jnp.arange(TOK_DEV, dtype=jnp.int32)[None, :]
        sum_q = jnp.zeros(block_shape, jnp.float32)
        sum_k = jnp.zeros(block_shape, jnp.float32)
        sum_v = jnp.zeros(block_shape, jnp.float32)
        for hop_index in range(GROUP_MOST):
            def one_block(index, hop=hop_index):
                key_index = (index - hop) % N_CP

                def live(unused):
                    return pair_terms(query_blocks[index], grad_blocks[index], log_blocks[index], delta_blocks[index], key_blocks[key_index], value_blocks[key_index], seq_ids[index], positions[index], seq_ids[key_index], positions[key_index], fire_w1, fire_b1, fire_w2)

                def dead(unused):
                    zero_block = jnp.zeros((TOK_DEV, HEADS, HEAD_DIM), jnp.float32)
                    return (zero_block, zero_block, zero_block, jnp.zeros((FIRE_HID,), jnp.float32), jnp.zeros((FIRE_HID,), jnp.float32), jnp.zeros((FIRE_HID, HEADS), jnp.float32))

                return lax.cond(seq_ids[index] == seq_ids[key_index], live, dead, 0)

            result = lax.map(one_block, jnp.arange(N_CP, dtype=jnp.int32))
            sum_q = sum_q + result[0]
            sum_k = sum_k + jnp.roll(result[1], -hop_index, axis=0)
            sum_v = sum_v + jnp.roll(result[2], -hop_index, axis=0)
            total_first = total_first + jnp.sum(result[3], axis=0)
            total_bias = total_bias + jnp.sum(result[4], axis=0)
            total_second = total_second + jnp.sum(result[5], axis=0)
        all_q.append(sum_q.reshape(TOKENS, WIDTH).astype(jnp.bfloat16))
        all_k.append(sum_k.reshape(TOKENS, WIDTH).astype(jnp.bfloat16))
        all_v.append(sum_v.reshape(TOKENS, WIDTH).astype(jnp.bfloat16))
    factor = (N_DP * TOKENS) ** -0.5
    return (jnp.stack(all_q), jnp.stack(all_k), jnp.stack(all_v), total_first * factor, total_bias * factor, total_second * factor)
```

```python
import jax
import jax.numpy as jnp
from jax import lax
from jax.experimental import pallas as pl
from jax.experimental.pallas import tpu as pltpu
from jax.sharding import PartitionSpec as P

GROUP_MOST = 4


fire_floor = 64.0


def shifted_2(block, axis, distance):
    devices = range(lax.axis_size(axis))
    route = [(i - distance, i) for i in devices if i - distance in devices]
    return lax.ppermute(block, axis, route)


def shifted_3(shard, axis, by):
    count = lax.axis_size(axis)
    return lax.ppermute(shard, axis, [(i, (i + by) % count) for i in range(count)])


def seat_of(length_row, device):
    ends = jnp.cumsum(length_row)
    sequence = jnp.sum((ends <= device).astype(jnp.int32))
    before = jnp.sum(
        jnp.where(jnp.arange(length_row.shape[0], dtype=jnp.int32) < sequence, length_row, 0)
    )
    return (sequence, device - before)


def pair_terms(
    query_heads,
    grad_heads,
    log_block,
    delta_block,
    key_heads,
    value_heads,
    query_seq,
    query_pos,
    key_seq,
    key_pos,
    fire_w1,
    fire_b1,
    fire_w2,
):
    highest = lax.Precision.HIGHEST
    scale_value = query_heads.shape[2] ** (-0.5)
    allowed = (query_seq == key_seq) & (key_pos[None, :] <= query_pos[:, None])
    distance = jnp.maximum(query_pos[:, None] - key_pos[None, :], 0).astype(jnp.float32)
    denom = jnp.log1p(jnp.maximum(query_pos.astype(jnp.float32), fire_floor))
    ratio = jnp.log1p(distance) / denom[:, None]
    hidden_pre = fire_w1[:, None, None] * ratio[None] + fire_b1[:, None, None]
    hidden_act = jnp.maximum(hidden_pre, 0.0)
    pair_bias = jnp.einsum("cqk,ch->hqk", hidden_act, fire_w2, precision=highest)
    scores = (
        jnp.einsum("qhd,khd->hqk", query_heads, key_heads, preferred_element_type=jnp.float32)
        * scale_value
        + pair_bias
    )
    shifted = jnp.where(allowed[None], scores - log_block.T[:, :, None], -1e30)
    prob_block = jnp.exp(shifted)
    dprob = jnp.einsum("qhd,khd->hqk", grad_heads, value_heads, preferred_element_type=jnp.float32)
    dscore = prob_block * (dprob - delta_block.T[:, :, None])
    prob_low = prob_block.astype(jnp.bfloat16)
    score_low = dscore.astype(jnp.bfloat16)
    grad_query = (
        jnp.einsum("hqk,khd->qhd", score_low, key_heads, preferred_element_type=jnp.float32)
        * scale_value
    )
    grad_key = (
        jnp.einsum("hqk,qhd->khd", score_low, query_heads, preferred_element_type=jnp.float32)
        * scale_value
    )
    grad_value = jnp.einsum(
        "hqk,qhd->khd", prob_low, grad_heads, preferred_element_type=jnp.float32
    )
    grad_second = jnp.einsum("hqk,cqk->ch", dscore, hidden_act, precision=highest)
    grad_act = jnp.einsum("hqk,ch->cqk", dscore, fire_w2, precision=highest)
    grad_pre = jnp.where(hidden_pre > 0, grad_act, 0.0)
    grad_first = jnp.sum(grad_pre * ratio[None], axis=(1, 2))
    grad_bias = jnp.sum(grad_pre, axis=(1, 2))
    return (grad_query, grad_key, grad_value, grad_first, grad_bias, grad_second)


def rotate_keys(key_value):
    return shifted_2(key_value, "cp", 1)


MESH = pl.DeviceIdType.MESH
NT = (((1,), (1,)), ((), ()))
NN = (((1,), (0,)), ((), ()))
TN = (((0,), (0,)), ((), ()))
MASKED = -1e30
BIAS_ROWS = 32
SUM_ROWS = 16


def exchange_kernel(
    q_ref,
    k_ref,
    v_ref,
    g_ref,
    stat_ref,
    start_ref,
    rden_ref,
    w1_ref,
    b1_ref,
    w2_ref,
    dq_ref,
    dk_ref,
    dv_ref,
    sums_ref,
    held,
    stats,
    pair,
    ratios,
    grads,
    acc,
    send_in,
    recv_in,
    send_stat,
    recv_stat,
    send_out,
    recv_out,
):
    parts = GROUP_MOST
    heads, tokens, size = held.shape[1:]
    rows = tokens // parts
    hidden = w1_ref.shape[0]
    scale_value = size ** (-0.5)
    me = lax.axis_index("cp")
    rank = lax.rem(me, parts)
    base = me - rank
    inputs = (q_ref, k_ref, v_ref, g_ref)
    results = (dq_ref, dk_ref, dv_ref)

    def peer_of(step):
        return lax.rem(rank + step, parts)

    def row_block(index):
        return pl.ds(pl.multiple_of(index * rows, rows), rows)

    def head_columns(part, head):
        return pl.ds(pl.multiple_of((part * heads + head) * size, size), size)

    def stat_copy(step):
        peer = peer_of(step)
        return pltpu.make_async_remote_copy(
            src_ref=stat_ref.at[peer],
            dst_ref=stats.at[rank],
            send_sem=send_stat.at[step - 1],
            recv_sem=recv_stat.at[step - 1],
            device_id={"cp": base + peer},
            device_id_type=MESH,
        )

    def in_copy(array, head, step):
        peer = peer_of(step)
        return pltpu.make_async_remote_copy(
            src_ref=inputs[array].at[:, head_columns(peer, head)],
            dst_ref=held.at[array, head, row_block(rank), :],
            send_sem=send_in.at[array, head, step - 1],
            recv_sem=recv_in.at[array, head, step - 1],
            device_id={"cp": base + peer},
            device_id_type=MESH,
        )

    def out_copy(array, head, step):
        peer = peer_of(step)
        return pltpu.make_async_remote_copy(
            src_ref=grads.at[array, head, row_block(peer), :],
            dst_ref=results[array].at[:, head_columns(rank, head)],
            send_sem=send_out.at[array, head, step - 1],
            recv_sem=recv_out.at[array, head, step - 1],
            device_id={"cp": base + peer},
            device_id_type=MESH,
        )

    barrier = pltpu.get_barrier_semaphore()
    for step in range(1, parts):
        pl.semaphore_signal(
            barrier, inc=1, device_id={"cp": base + peer_of(step)}, device_id_type=MESH
        )
    pl.semaphore_wait(barrier, parts - 1)

    for step in range(1, parts):
        stat_copy(step).start()

    def send_head(head, carry):
        for step in (2, 1, 3):
            for array in range(4):
                in_copy(array, head, step).start()
        return carry

    lax.fori_loop(0, heads, send_head, 0)

    stats[rank] = stat_ref[rank]

    def own_head(head, carry):
        for array in range(4):
            held[array, head, row_block(rank), :] = inputs[array][:, head_columns(rank, head)]
        return carry

    lax.fori_loop(0, heads, own_head, 0)

    def bias_column(block, carry):
        columns = row_block(block)
        start = start_ref[:, columns]
        rden = rden_ref[:, columns]

        def bias_rows(chunk, carry):
            at = pl.ds(pl.multiple_of(chunk * BIAS_ROWS, BIAS_ROWS), BIAS_ROWS)
            key_at = chunk * BIAS_ROWS + lax.broadcasted_iota(jnp.int32, (BIAS_ROWS, rows), 0)
            query_at = block * rows + lax.broadcasted_iota(jnp.int32, (BIAS_ROWS, rows), 1)
            allowed = (key_at >= start) & (key_at <= query_at)
            distance = jnp.maximum(query_at - key_at, 0).astype(jnp.float32)
            ratio = jnp.log(1.0 + distance) * rden
            ratios[at, columns] = ratio
            totals = [jnp.zeros((BIAS_ROWS, rows), jnp.float32) for _ in range(heads)]
            for unit in range(hidden):
                act = jnp.maximum(ratio * w1_ref[unit] + b1_ref[unit], 0.0)
                for head in range(heads):
                    totals[head] = totals[head] + act * w2_ref[unit, head]
            for head in range(heads):
                pair[head, at, columns] = jnp.where(allowed, totals[head], MASKED)
            return carry

        return lax.fori_loop(0, (block + 1) * (rows // BIAS_ROWS), bias_rows, carry)

    lax.fori_loop(0, parts, bias_column, 0)
    half = 2 * rows
    for head in range(heads):
        for first in range(0, parts, 2):
            pair[head, (first + 1) * rows : (first + 2) * rows, first * rows : (first + 1) * rows] = (
                jnp.full((rows, rows), MASKED, jnp.float32)
            )
    acc[...] = jnp.zeros_like(acc)

    for step in range(1, parts):
        stat_copy(step).wait_recv()

    def one_head(head, carry):
        for step in (2, 1, 3):
            for array in range(4):
                in_copy(array, head, step).wait_recv()
        log_row = jnp.concatenate(
            [stats[part, pl.ds(head, 1), :] for part in range(parts)], axis=1
        )
        delta_row = jnp.concatenate(
            [stats[part, pl.ds(8 + head, 1), :] for part in range(parts)], axis=1
        )

        def dot(a, b, dims):
            return lax.dot_general(a, b, dims, preferred_element_type=jnp.float32)

        dq = [None, None]
        dk = [None, None]
        dv = [None, None]

        def plus(total, term):
            return term if total is None else total + term

        for kt, qt in ((0, 0), (0, 1), (1, 1)):
            krows = slice(kt * half, (kt + 1) * half)
            qrows = slice(qt * half, (qt + 1) * half)
            q = held[0, head, qrows, :]
            k = held[1, head, krows, :]
            v = held[2, head, krows, :]
            g = held[3, head, qrows, :]
            scores = dot(k, q, NT) * scale_value + pair[head, krows, qrows]
            prob = jnp.exp(scores - log_row[:, qrows])
            dscore = prob * (dot(v, g, NT) - delta_row[:, qrows])
            pair[head, krows, qrows] = dscore
            prob_low = prob.astype(jnp.bfloat16)
            score_low = dscore.astype(jnp.bfloat16)
            dv[kt] = plus(dv[kt], dot(prob_low, g, NN))
            dk[kt] = plus(dk[kt], dot(score_low, q, NN))
            dq[qt] = plus(dq[qt], dot(score_low, k, TN))
        for tile in range(2):
            trows = slice(tile * half, (tile + 1) * half)
            grads[0, head, trows, :] = (dq[tile] * scale_value).astype(jnp.bfloat16)
            grads[1, head, trows, :] = (dk[tile] * scale_value).astype(jnp.bfloat16)
            grads[2, head, trows, :] = dv[tile].astype(jnp.bfloat16)
        for step in (2, 1, 3):
            for array in range(3):
                out_copy(array, head, step).start()
        for array in range(3):
            results[array][:, head_columns(rank, head)] = grads[array, head, row_block(rank), :]
        return carry

    lax.fori_loop(0, heads, one_head, 0)

    def sum_column(block, carry):
        columns = row_block(block)

        def sum_rows(chunk, carry):
            at = pl.ds(pl.multiple_of(chunk * SUM_ROWS, SUM_ROWS), SUM_ROWS)
            ratio = ratios[at, columns]
            flat = [pair[head, at, columns] for head in range(heads)]
            tilted = [term * ratio for term in flat]
            for unit in range(hidden):
                live = ratio * w1_ref[unit] > -b1_ref[unit]
                for head in range(heads):
                    for kind, term in ((0, flat[head]), (1, tilted[head])):
                        kept = jnp.where(live, term, 0.0)
                        part = kept[0:8]
                        for row in range(8, SUM_ROWS, 8):
                            part = part + kept[row : row + 8]
                        acc[kind, head, unit] += part
            return carry

        return lax.fori_loop(0, (block + 1) * (rows // SUM_ROWS), sum_rows, carry)

    lax.fori_loop(0, parts, sum_column, 0)
    for kind in range(2):
        for head in range(heads):
            sums_ref[kind, head] = jnp.sum(acc[kind, head], axis=1)

    def drain_head(head, carry):
        for step in (2, 1, 3):
            for array in range(4):
                in_copy(array, head, step).wait_send()
            for array in range(3):
                out_copy(array, head, step).wait()
        return carry

    lax.fori_loop(0, heads, drain_head, 0)
    for step in range(1, parts):
        stat_copy(step).wait_send()


def by_heads(queries, keys, values, outputs, d_out, log_norm, lengths, fire_w1, fire_b1, fire_w2):
    rows_dev = queries.shape[1]
    heads_count = log_norm.shape[2]
    feature_count = queries.shape[2]
    head_size = feature_count // heads_count
    cp_count = lax.axis_size("cp")
    parts = GROUP_MOST
    heads = heads_count // parts
    hidden = fire_w1.shape[0]
    tokens = parts * rows_dev
    me = lax.axis_index("cp")
    rank = lax.rem(me, parts)
    base = me - rank
    delta = jnp.einsum(
        "qhd,qhd->hq",
        d_out[0].reshape(rows_dev, heads_count, head_size),
        outputs[0].reshape(rows_dev, heads_count, head_size),
        preferred_element_type=jnp.float32,
    )
    pad = ((0, 0), (0, 8 - heads), (0, 0))
    stat = jnp.concatenate(
        [
            jnp.pad(log_norm[0].T.reshape(parts, heads, rows_dev), pad),
            jnp.pad(delta.reshape(parts, heads, rows_dev), pad),
        ],
        axis=1,
    )
    ends = jnp.cumsum(lengths[0])
    begins = ends - lengths[0]
    blocks = base + jnp.arange(parts, dtype=jnp.int32)
    mine = (begins[None, :] <= blocks[:, None]) & (blocks[:, None] < ends[None, :])
    begin = (jnp.sum(jnp.where(mine, begins[None, :], 0), axis=1) - base) * rows_dev
    start = jnp.repeat(begin, rows_dev)[None, :]
    position = (jnp.arange(tokens, dtype=jnp.int32)[None, :] - start).astype(jnp.float32)
    rden = 1.0 / jnp.log1p(jnp.maximum(position, fire_floor))
    w2_mine = lax.dynamic_slice(fire_w2, (0, rank * heads), (hidden, heads))

    vmem = pl.BlockSpec(memory_space=pltpu.VMEM)
    smem = pl.BlockSpec(memory_space=pltpu.SMEM)
    low = jnp.bfloat16
    block = jax.ShapeDtypeStruct((rows_dev, feature_count), low)
    steps = parts - 1
    dma = pltpu.SemaphoreType.DMA
    grad_q, grad_k, grad_v, sums = pl.pallas_call(
        exchange_kernel,
        out_shape=(
            block,
            block,
            block,
            jax.ShapeDtypeStruct((2, heads, hidden, 128), jnp.float32),
        ),
        in_specs=[vmem] * 7 + [smem] * 3,
        out_specs=(vmem,) * 4,
        scratch_shapes=[
            pltpu.VMEM((4, heads, tokens, head_size), low),
            pltpu.VMEM((parts, 16, rows_dev), jnp.float32),
            pltpu.VMEM((heads, tokens, tokens), jnp.float32),
            pltpu.VMEM((tokens, tokens), jnp.float32),
            pltpu.VMEM((3, heads, tokens, head_size), low),
            pltpu.VMEM((2, heads, hidden, 8, 128), jnp.float32),
            dma((4, heads, steps)),
            dma((4, heads, steps)),
            dma((steps,)),
            dma((steps,)),
            dma((3, heads, steps)),
            dma((3, heads, steps)),
        ],
        compiler_params=pltpu.CompilerParams(
            collective_id=0, has_side_effects=True, vmem_limit_bytes=48 * 2**20
        ),
    )(queries[0], keys[0], values[0], d_out[0], stat, start, rden, fire_w1, fire_b1, w2_mine)
    sums = jnp.sum(sums, axis=3)
    flat, tilted = sums[0].T, sums[1].T
    second = jnp.zeros((hidden, heads_count), jnp.float32)
    second = lax.dynamic_update_slice(
        second, fire_w1[:, None] * tilted + fire_b1[:, None] * flat, (0, rank * heads)
    )
    first = jnp.sum(w2_mine * tilted, axis=1)
    bias_sum = jnp.sum(w2_mine * flat, axis=1)
    joined = jnp.concatenate([second, first[:, None], bias_sum[:, None]], axis=1)
    factor = (lax.axis_size("dp") * cp_count * rows_dev) ** (-0.5)
    joined = lax.psum(joined, ("cp", "dp")) * factor
    return (
        grad_q[None],
        grad_k[None],
        grad_v[None],
        joined[:, heads_count],
        joined[:, heads_count + 1],
        joined[:, :heads_count],
    )


def on_device(queries, keys, values, outputs, d_out, log_norm, lengths, fire_w1, fire_b1, fire_w2):
    rows_dev = queries.shape[1]
    heads_count = log_norm.shape[2]
    feature_count = queries.shape[2]
    head_size = feature_count // heads_count
    cp_count = lax.axis_size("cp")
    my_index = lax.axis_index("cp")
    length_row = lengths[0]
    reach = GROUP_MOST - 1
    query_heads = queries[0].reshape(rows_dev, heads_count, head_size)
    key_heads = keys[0].reshape(rows_dev, heads_count, head_size)
    value_heads = values[0].reshape(rows_dev, heads_count, head_size)
    grad_heads = d_out[0].reshape(rows_dev, heads_count, head_size)
    out_heads = outputs[0].reshape(rows_dev, heads_count, head_size)
    log_block = log_norm[0]
    delta_block = jnp.einsum(
        "qhd,qhd->qh", grad_heads, out_heads, preferred_element_type=jnp.float32
    )
    token_index = jnp.arange(rows_dev, dtype=jnp.int32)

    def seat_positions(device):
        sequence, offset = seat_of(length_row, device)
        return (sequence, offset * rows_dev + token_index)

    my_seq, my_pos = seat_positions(my_index)
    local = pair_terms(
        query_heads,
        grad_heads,
        log_block,
        delta_block,
        key_heads,
        value_heads,
        my_seq,
        my_pos,
        my_seq,
        my_pos,
        fire_w1,
        fire_b1,
        fire_w2,
    )
    key_value = jnp.stack([key_heads, value_heads])

    def carried_hop(hop_index, carry):
        moving_kv, moving_grads, grad_q, first, bias_sum, second = carry
        moving_kv = rotate_keys(moving_kv)
        moving_grads = shifted_3(moving_grads, "cp", 1)
        key_seq, key_pos = seat_positions((my_index - hop_index) % cp_count)
        terms = pair_terms(
            query_heads,
            grad_heads,
            log_block,
            delta_block,
            moving_kv[0],
            moving_kv[1],
            my_seq,
            my_pos,
            key_seq,
            key_pos,
            fire_w1,
            fire_b1,
            fire_w2,
        )
        moving_grads = moving_grads + jnp.stack([terms[1], terms[2]])
        return (
            moving_kv,
            moving_grads,
            grad_q + terms[0],
            first + terms[3],
            bias_sum + terms[4],
            second + terms[5],
        )

    start = (key_value, jnp.stack([local[1], local[2]]), local[0], local[3], local[4], local[5])
    result = lax.fori_loop(1, GROUP_MOST, carried_hop, start)
    grad_q, first, bias_sum, second = (result[2], result[3], result[4], result[5])
    home_grads = shifted_3(result[1].astype(jnp.bfloat16), "cp", -reach).astype(jnp.float32)
    grad_k, grad_v = (home_grads[0], home_grads[1])
    first, bias_sum, second = lax.psum((first, bias_sum, second), ("cp", "dp"))
    factor = (lax.axis_size("dp") * cp_count * rows_dev) ** (-0.5)
    out_shape = (1, rows_dev, feature_count)
    return (
        grad_q.reshape(out_shape).astype(jnp.bfloat16),
        grad_k.reshape(out_shape).astype(jnp.bfloat16),
        grad_v.reshape(out_shape).astype(jnp.bfloat16),
        first * factor,
        bias_sum * factor,
        second * factor,
    )


def solution(mesh):
    placed = (
        P("dp", "cp", None),
        P("dp", "cp", None),
        P("dp", "cp", None),
        P("dp", "cp", None),
        P("dp", "cp", None),
        P("dp", "cp", None),
        P("dp", None),
        P(),
        P(),
        P(),
    )
    plan = by_heads if mesh.shape["cp"] == 2 * GROUP_MOST else on_device
    return jax.shard_map(
        plan,
        mesh=mesh,
        in_specs=placed,
        out_specs=(P("dp", "cp", None), P("dp", "cp", None), P("dp", "cp", None), P(), P(), P()),
        check_vma=False,
    )
```

```python
import jax
import jax.numpy as jnp
from jax import lax
from jax.experimental import pallas as pl
from jax.experimental.pallas import tpu as pltpu
from jax.sharding import PartitionSpec as P

GROUP_MOST = 4


fire_floor = 64.0


def shifted_2(block, axis, distance):
    devices = range(lax.axis_size(axis))
    route = [(i - distance, i) for i in devices if i - distance in devices]
    return lax.ppermute(block, axis, route)


def shifted_3(shard, axis, by):
    count = lax.axis_size(axis)
    return lax.ppermute(shard, axis, [(i, (i + by) % count) for i in range(count)])


def seat_of(length_row, device):
    ends = jnp.cumsum(length_row)
    sequence = jnp.sum((ends <= device).astype(jnp.int32))
    before = jnp.sum(
        jnp.where(jnp.arange(length_row.shape[0], dtype=jnp.int32) < sequence, length_row, 0)
    )
    return (sequence, device - before)


def pair_terms(
    query_heads,
    grad_heads,
    log_block,
    delta_block,
    key_heads,
    value_heads,
    query_seq,
    query_pos,
    key_seq,
    key_pos,
    fire_w1,
    fire_b1,
    fire_w2,
):
    highest = lax.Precision.HIGHEST
    scale_value = query_heads.shape[2] ** (-0.5)
    allowed = (query_seq == key_seq) & (key_pos[None, :] <= query_pos[:, None])
    distance = jnp.maximum(query_pos[:, None] - key_pos[None, :], 0).astype(jnp.float32)
    denom = jnp.log1p(jnp.maximum(query_pos.astype(jnp.float32), fire_floor))
    ratio = jnp.log1p(distance) / denom[:, None]
    hidden_pre = fire_w1[:, None, None] * ratio[None] + fire_b1[:, None, None]
    hidden_act = jnp.maximum(hidden_pre, 0.0)
    pair_bias = jnp.einsum("cqk,ch->hqk", hidden_act, fire_w2, precision=highest)
    scores = (
        jnp.einsum("qhd,khd->hqk", query_heads, key_heads, preferred_element_type=jnp.float32)
        * scale_value
        + pair_bias
    )
    shifted = jnp.where(allowed[None], scores - log_block.T[:, :, None], -1e30)
    prob_block = jnp.exp(shifted)
    dprob = jnp.einsum("qhd,khd->hqk", grad_heads, value_heads, preferred_element_type=jnp.float32)
    dscore = prob_block * (dprob - delta_block.T[:, :, None])
    prob_low = prob_block.astype(jnp.bfloat16)
    score_low = dscore.astype(jnp.bfloat16)
    grad_query = (
        jnp.einsum("hqk,khd->qhd", score_low, key_heads, preferred_element_type=jnp.float32)
        * scale_value
    )
    grad_key = (
        jnp.einsum("hqk,qhd->khd", score_low, query_heads, preferred_element_type=jnp.float32)
        * scale_value
    )
    grad_value = jnp.einsum(
        "hqk,qhd->khd", prob_low, grad_heads, preferred_element_type=jnp.float32
    )
    grad_second = jnp.einsum("hqk,cqk->ch", dscore, hidden_act, precision=highest)
    grad_act = jnp.einsum("hqk,ch->cqk", dscore, fire_w2, precision=highest)
    grad_pre = jnp.where(hidden_pre > 0, grad_act, 0.0)
    grad_first = jnp.sum(grad_pre * ratio[None], axis=(1, 2))
    grad_bias = jnp.sum(grad_pre, axis=(1, 2))
    return (grad_query, grad_key, grad_value, grad_first, grad_bias, grad_second)


def rotate_keys(key_value):
    return shifted_2(key_value, "cp", 1)


MESH = pl.DeviceIdType.MESH
NT = (((1,), (1,)), ((), ()))
NN = (((1,), (0,)), ((), ()))
TN = (((0,), (0,)), ((), ()))
MASKED = -1e30
BIAS_ROWS = 32
SUM_ROWS = 32


def exchange_kernel(
    q_ref,
    k_ref,
    v_ref,
    g_ref,
    o_ref,
    log_ref,
    lengths_ref,
    w1_ref,
    b1_ref,
    w2_ref,
    dq_ref,
    dk_ref,
    dv_ref,
    sums_ref,
    held,
    own_g,
    own_o,
    padded,
    stats,
    pair,
    ratios,
    grads,
    acc,
    lanes,
    cp_slots,
    dp_slots,
    own_sem,
    delta_sem,
    send_in,
    recv_in,
    send_stat,
    recv_stat,
    send_out,
    recv_out,
    send_cp,
    recv_cp,
    send_dp,
    recv_dp,
):
    parts = GROUP_MOST
    heads, tokens, size = held.shape[1:]
    rows = tokens // parts
    hidden = w1_ref.shape[0]
    heads_count = heads * parts
    delta_at = stats.shape[1] // 2
    cp_count, dp_count = cp_slots.shape[0], dp_slots.shape[0]
    scale_value = size ** (-0.5)
    me = lax.axis_index("cp")
    my_dp = lax.axis_index("dp")
    rank = lax.rem(me, parts)
    base = me - rank
    inputs = (q_ref, k_ref, v_ref, g_ref)
    results = (dq_ref, dk_ref, dv_ref)

    def dot(a, b, dims):
        return lax.dot_general(a, b, dims, preferred_element_type=jnp.float32)

    def peer_of(step):
        return lax.rem(rank + step, parts)

    def row_block(index):
        return pl.ds(pl.multiple_of(index * rows, rows), rows)

    def head_columns(part, head):
        return pl.ds(pl.multiple_of((part * heads + head) * size, size), size)

    def stat_copy(step):
        return pltpu.make_async_remote_copy(
            src_ref=stats.at[rank],
            dst_ref=stats.at[rank],
            send_sem=send_stat.at[step - 1],
            recv_sem=recv_stat.at[step - 1],
            device_id={"cp": base + peer_of(step)},
            device_id_type=MESH,
        )

    def in_copy(array, head, step):
        peer = peer_of(step)
        return pltpu.make_async_remote_copy(
            src_ref=inputs[array].at[:, head_columns(peer, head)],
            dst_ref=held.at[array, head, row_block(rank), :],
            send_sem=send_in.at[array, head, step - 1],
            recv_sem=recv_in.at[array, head, step - 1],
            device_id={"cp": base + peer},
            device_id_type=MESH,
        )

    def own_copy(array, head):
        return pltpu.make_async_copy(
            inputs[array].at[:, head_columns(rank, head)],
            held.at[array, head, row_block(rank), :],
            own_sem.at[array, head],
        )

    def out_copy(array, head, step):
        peer = peer_of(step)
        return pltpu.make_async_remote_copy(
            src_ref=grads.at[array, head, row_block(peer), :],
            dst_ref=results[array].at[:, head_columns(rank, head)],
            send_sem=send_out.at[array, head, step - 1],
            recv_sem=recv_out.at[array, head, step - 1],
            device_id={"cp": base + peer},
            device_id_type=MESH,
        )

    def cp_copy(step):
        return pltpu.make_async_remote_copy(
            src_ref=cp_slots.at[me],
            dst_ref=cp_slots.at[me],
            send_sem=send_cp.at[step - 1],
            recv_sem=recv_cp.at[step - 1],
            device_id={"cp": lax.rem(me + step, cp_count)},
            device_id_type=MESH,
        )

    def dp_copy(step):
        return pltpu.make_async_remote_copy(
            src_ref=dp_slots.at[my_dp],
            dst_ref=dp_slots.at[my_dp],
            send_sem=send_dp.at[step - 1],
            recv_sem=recv_dp.at[step - 1],
            device_id={"dp": lax.rem(my_dp + step, dp_count)},
            device_id_type=MESH,
        )

    delta_copies = (
        pltpu.make_async_copy(g_ref, own_g, delta_sem.at[0]),
        pltpu.make_async_copy(o_ref, own_o, delta_sem.at[1]),
    )
    for copy in delta_copies:
        copy.start()

    barrier = pltpu.get_barrier_semaphore()
    for step in range(1, cp_count):
        pl.semaphore_signal(
            barrier, inc=1, device_id={"cp": lax.rem(me + step, cp_count)}, device_id_type=MESH
        )
    for step in range(1, dp_count):
        pl.semaphore_signal(
            barrier, inc=1, device_id={"dp": lax.rem(my_dp + step, dp_count)}, device_id_type=MESH
        )
    pl.semaphore_wait(barrier, cp_count + dp_count - 2)

    def send_head(head, carry):
        for step in (2, 1, 3):
            for array in range(4):
                in_copy(array, head, step).start()
        for array in range(4):
            own_copy(array, head).start()
        return carry

    early = 2
    lax.fori_loop(0, early, send_head, 0)

    padded[...] = jnp.zeros_like(padded)
    padded[:, 0:heads_count] = log_ref[...]
    stats[rank] = jnp.zeros(stats.shape[1:], jnp.float32)
    stats[rank, 0:delta_at, :] = padded[...].T[0:delta_at]
    for copy in delta_copies:
        copy.wait()
    ones = jnp.ones((8, 2 * size), jnp.bfloat16)

    def delta_head(head, carry):
        columns = pl.ds(pl.multiple_of(head * size, size), size)
        product = own_g[:, columns].astype(jnp.float32) * own_o[:, columns].astype(jnp.float32)
        high = product.astype(jnp.bfloat16)
        rest = (product - high.astype(jnp.float32)).astype(jnp.bfloat16)
        row = dot(ones, jnp.concatenate([high, rest], axis=1), NT)
        stats[rank, pl.ds(delta_at + head, 1), :] = row[0:1]
        return carry

    lax.fori_loop(0, heads_count, delta_head, 0)
    for step in range(1, parts):
        stat_copy(step).start()
    lax.fori_loop(early, heads, send_head, 0)

    def bias_column(block, carry):
        columns = row_block(block)
        start = jnp.int32(0)
        end = jnp.int32(0)
        for index in range(lengths_ref.shape[1]):
            start = jnp.where(end <= base + block, end, start)
            end = end + lengths_ref[0, index]
        start = (start - base) * rows
        query_row = block * rows + lax.broadcasted_iota(jnp.int32, (1, rows), 1)
        position = (query_row - start).astype(jnp.float32)
        rden = 1.0 / jnp.log(1.0 + jnp.maximum(position, fire_floor))

        def bias_rows(chunk, carry):
            at = pl.ds(pl.multiple_of(chunk * BIAS_ROWS, BIAS_ROWS), BIAS_ROWS)
            key_at = chunk * BIAS_ROWS + lax.broadcasted_iota(jnp.int32, (BIAS_ROWS, rows), 0)
            query_at = block * rows + lax.broadcasted_iota(jnp.int32, (BIAS_ROWS, rows), 1)
            allowed = (key_at >= start) & (key_at <= query_at)
            distance = jnp.maximum(query_at - key_at, 0).astype(jnp.float32)
            ratio = jnp.log(1.0 + distance) * rden
            ratios[at, columns] = ratio
            totals = [jnp.zeros((BIAS_ROWS, rows), jnp.float32) for _ in range(heads)]
            for unit in range(hidden):
                act = jnp.maximum(ratio * w1_ref[unit] + b1_ref[unit], 0.0)
                for head in range(heads):
                    totals[head] = totals[head] + act * w2_ref[unit, rank * heads + head]
            for head in range(heads):
                pair[head, at, columns] = jnp.where(allowed, totals[head], MASKED)
            return carry

        return lax.fori_loop(0, (block + 1) * (rows // BIAS_ROWS), bias_rows, carry)

    lax.fori_loop(0, parts, bias_column, 0)
    half = 2 * rows
    for head in range(heads):
        for first in range(0, parts, 2):
            pair[head, (first + 1) * rows : (first + 2) * rows, first * rows : (first + 1) * rows] = (
                jnp.full((rows, rows), MASKED, jnp.float32)
            )
    acc[...] = jnp.zeros_like(acc)

    for step in range(1, parts):
        stat_copy(step).wait_recv()

    def one_head(head, carry):
        for array in range(4):
            own_copy(array, head).wait()
        for step in (2, 1, 3):
            for array in range(4):
                in_copy(array, head, step).wait_recv()
        at = rank * heads + head
        log_row = jnp.concatenate([stats[part, pl.ds(at, 1), :] for part in range(parts)], axis=1)
        delta_row = jnp.concatenate(
            [stats[part, pl.ds(delta_at + at, 1), :] for part in range(parts)], axis=1
        )

        dq = [None, None]
        dk = [None, None]
        dv = [None, None]

        def plus(total, term):
            return term if total is None else total + term

        for kt, qt in ((0, 0), (0, 1), (1, 1)):
            krows = slice(kt * half, (kt + 1) * half)
            qrows = slice(qt * half, (qt + 1) * half)
            q = held[0, head, qrows, :]
            k = held[1, head, krows, :]
            v = held[2, head, krows, :]
            g = held[3, head, qrows, :]
            scores = dot(k, q, NT) * scale_value + pair[head, krows, qrows]
            prob = jnp.exp(scores - log_row[:, qrows])
            dscore = prob * (dot(v, g, NT) - delta_row[:, qrows])
            pair[head, krows, qrows] = dscore
            prob_low = prob.astype(jnp.bfloat16)
            score_low = dscore.astype(jnp.bfloat16)
            dv[kt] = plus(dv[kt], dot(prob_low, g, NN))
            dk[kt] = plus(dk[kt], dot(score_low, q, NN))
            dq[qt] = plus(dq[qt], dot(score_low, k, TN))
        for tile in range(2):
            trows = slice(tile * half, (tile + 1) * half)
            grads[0, head, trows, :] = (dq[tile] * scale_value).astype(jnp.bfloat16)
            grads[1, head, trows, :] = (dk[tile] * scale_value).astype(jnp.bfloat16)
            grads[2, head, trows, :] = dv[tile].astype(jnp.bfloat16)
        for step in (2, 1, 3):
            for array in range(3):
                out_copy(array, head, step).start()
        for array in range(3):
            results[array][:, head_columns(rank, head)] = grads[array, head, row_block(rank), :]
        return carry

    def sum_heads(some):
        def sum_column(block, carry):
            columns = row_block(block)

            def sum_rows(chunk, carry):
                at = pl.ds(pl.multiple_of(chunk * SUM_ROWS, SUM_ROWS), SUM_ROWS)
                ratio = ratios[at, columns]
                flat = {head: pair[head, at, columns] for head in some}
                tilted = {head: flat[head] * ratio for head in some}
                for unit in range(hidden):
                    live = ratio * w1_ref[unit] > -b1_ref[unit]
                    for head in some:
                        for kind, term in ((0, flat[head]), (1, tilted[head])):
                            kept = jnp.where(live, term, 0.0)
                            part = kept[0:8]
                            for row in range(8, SUM_ROWS, 8):
                                part = part + kept[row : row + 8]
                            acc[kind, head, unit] += part
                return carry

            return lax.fori_loop(0, (block + 1) * (rows // SUM_ROWS), sum_rows, carry)

        lax.fori_loop(0, parts, sum_column, 0)

    lax.fori_loop(0, early, one_head, 0)
    sum_heads(range(0, early))
    lax.fori_loop(early, heads, one_head, 0)
    sum_heads(range(early, heads))

    for unit in range(hidden):
        first = jnp.zeros((8, 128), jnp.float32)
        bias_sum = jnp.zeros((8, 128), jnp.float32)
        for head in range(heads):
            flat, tilted = acc[0, head, unit], acc[1, head, unit]
            weight = w2_ref[unit, rank * heads + head]
            first = first + tilted * weight
            bias_sum = bias_sum + flat * weight
            second = tilted * w1_ref[unit] + flat * b1_ref[unit]
            lanes[head, unit : unit + 1, :] = jnp.sum(second, axis=0, keepdims=True)
        lanes[heads, unit : unit + 1, :] = jnp.sum(first, axis=0, keepdims=True)
        lanes[heads + 1, unit : unit + 1, :] = jnp.sum(bias_sum, axis=0, keepdims=True)
    lane = lax.broadcasted_iota(jnp.int32, (hidden, 128), 1)
    message = jnp.zeros((hidden, 128), jnp.float32)
    for index in range(heads + 2):
        place = rank * heads + index if index < heads else heads_count + index - heads
        column = jnp.sum(lanes[index], axis=1, keepdims=True)
        message = jnp.where(lane == place, column, message)
    cp_slots[me] = message
    for step in range(1, cp_count):
        cp_copy(step).start()
    for step in range(1, cp_count):
        cp_copy(step).wait()
    total = cp_slots[0]
    for index in range(1, cp_count):
        total = total + cp_slots[index]
    dp_slots[my_dp] = total
    for step in range(1, dp_count):
        dp_copy(step).start()
    for step in range(1, dp_count):
        dp_copy(step).wait()
    total = dp_slots[0]
    for index in range(1, dp_count):
        total = total + dp_slots[index]
    sums_ref[...] = total * (dp_count * cp_count * rows) ** (-0.5)

    def drain_head(head, carry):
        for step in (2, 1, 3):
            for array in range(4):
                in_copy(array, head, step).wait_send()
            for array in range(3):
                out_copy(array, head, step).wait()
        return carry

    lax.fori_loop(0, heads, drain_head, 0)
    for step in range(1, parts):
        stat_copy(step).wait_send()


def by_heads(queries, keys, values, outputs, d_out, log_norm, lengths, fire_w1, fire_b1, fire_w2):
    rows_dev = queries.shape[1]
    heads_count = log_norm.shape[2]
    feature_count = queries.shape[2]
    head_size = feature_count // heads_count
    cp_count, dp_count = lax.axis_size("cp"), lax.axis_size("dp")
    parts = GROUP_MOST
    heads = heads_count // parts
    hidden = fire_w1.shape[0]
    tokens = parts * rows_dev
    stat_rows = 2 * (-(-heads_count // 8) * 8)

    anywhere = pl.BlockSpec(memory_space=pl.ANY)
    vmem = pl.BlockSpec(memory_space=pltpu.VMEM)
    smem = pl.BlockSpec(memory_space=pltpu.SMEM)
    low = jnp.bfloat16
    wide = jnp.float32
    block = jax.ShapeDtypeStruct((rows_dev, feature_count), low)
    steps = parts - 1
    dma = pltpu.SemaphoreType.DMA
    grad_q, grad_k, grad_v, sums = pl.pallas_call(
        exchange_kernel,
        out_shape=(block, block, block, jax.ShapeDtypeStruct((hidden, 128), wide)),
        in_specs=[anywhere] * 5 + [vmem] + [smem] * 4,
        out_specs=(vmem,) * 4,
        scratch_shapes=[
            pltpu.VMEM((4, heads, tokens, head_size), low),
            pltpu.VMEM((rows_dev, feature_count), low),
            pltpu.VMEM((rows_dev, feature_count), low),
            pltpu.VMEM((rows_dev, 128), wide),
            pltpu.VMEM((parts, stat_rows, rows_dev), wide),
            pltpu.VMEM((heads, tokens, tokens), wide),
            pltpu.VMEM((tokens, tokens), wide),
            pltpu.VMEM((3, heads, tokens, head_size), low),
            pltpu.VMEM((2, heads, hidden, 8, 128), wide),
            pltpu.VMEM((heads + 2, hidden, 128), wide),
            pltpu.VMEM((cp_count, hidden, 128), wide),
            pltpu.VMEM((dp_count, hidden, 128), wide),
            dma((4, heads)),
            dma((2,)),
            dma((4, heads, steps)),
            dma((4, heads, steps)),
            dma((steps,)),
            dma((steps,)),
            dma((3, heads, steps)),
            dma((3, heads, steps)),
            dma((cp_count - 1,)),
            dma((cp_count - 1,)),
            dma((dp_count - 1,)),
            dma((dp_count - 1,)),
        ],
        compiler_params=pltpu.CompilerParams(
            collective_id=0, has_side_effects=True, vmem_limit_bytes=48 * 2**20
        ),
    )(
        queries[0],
        keys[0],
        values[0],
        d_out[0],
        outputs[0],
        log_norm[0],
        lengths,
        fire_w1,
        fire_b1,
        fire_w2,
    )
    return (
        grad_q[None],
        grad_k[None],
        grad_v[None],
        sums[:, heads_count],
        sums[:, heads_count + 1],
        sums[:, :heads_count],
    )


def on_device(queries, keys, values, outputs, d_out, log_norm, lengths, fire_w1, fire_b1, fire_w2):
    rows_dev = queries.shape[1]
    heads_count = log_norm.shape[2]
    feature_count = queries.shape[2]
    head_size = feature_count // heads_count
    cp_count = lax.axis_size("cp")
    my_index = lax.axis_index("cp")
    length_row = lengths[0]
    reach = GROUP_MOST - 1
    query_heads = queries[0].reshape(rows_dev, heads_count, head_size)
    key_heads = keys[0].reshape(rows_dev, heads_count, head_size)
    value_heads = values[0].reshape(rows_dev, heads_count, head_size)
    grad_heads = d_out[0].reshape(rows_dev, heads_count, head_size)
    out_heads = outputs[0].reshape(rows_dev, heads_count, head_size)
    log_block = log_norm[0]
    delta_block = jnp.einsum(
        "qhd,qhd->qh", grad_heads, out_heads, preferred_element_type=jnp.float32
    )
    token_index = jnp.arange(rows_dev, dtype=jnp.int32)

    def seat_positions(device):
        sequence, offset = seat_of(length_row, device)
        return (sequence, offset * rows_dev + token_index)

    my_seq, my_pos = seat_positions(my_index)
    local = pair_terms(
        query_heads,
        grad_heads,
        log_block,
        delta_block,
        key_heads,
        value_heads,
        my_seq,
        my_pos,
        my_seq,
        my_pos,
        fire_w1,
        fire_b1,
        fire_w2,
    )
    key_value = jnp.stack([key_heads, value_heads])

    def carried_hop(hop_index, carry):
        moving_kv, moving_grads, grad_q, first, bias_sum, second = carry
        moving_kv = rotate_keys(moving_kv)
        moving_grads = shifted_3(moving_grads, "cp", 1)
        key_seq, key_pos = seat_positions((my_index - hop_index) % cp_count)
        terms = pair_terms(
            query_heads,
            grad_heads,
            log_block,
            delta_block,
            moving_kv[0],
            moving_kv[1],
            my_seq,
            my_pos,
            key_seq,
            key_pos,
            fire_w1,
            fire_b1,
            fire_w2,
        )
        moving_grads = moving_grads + jnp.stack([terms[1], terms[2]])
        return (
            moving_kv,
            moving_grads,
            grad_q + terms[0],
            first + terms[3],
            bias_sum + terms[4],
            second + terms[5],
        )

    start = (key_value, jnp.stack([local[1], local[2]]), local[0], local[3], local[4], local[5])
    result = lax.fori_loop(1, GROUP_MOST, carried_hop, start)
    grad_q, first, bias_sum, second = (result[2], result[3], result[4], result[5])
    home_grads = shifted_3(result[1].astype(jnp.bfloat16), "cp", -reach).astype(jnp.float32)
    grad_k, grad_v = (home_grads[0], home_grads[1])
    first, bias_sum, second = lax.psum((first, bias_sum, second), ("cp", "dp"))
    factor = (lax.axis_size("dp") * cp_count * rows_dev) ** (-0.5)
    out_shape = (1, rows_dev, feature_count)
    return (
        grad_q.reshape(out_shape).astype(jnp.bfloat16),
        grad_k.reshape(out_shape).astype(jnp.bfloat16),
        grad_v.reshape(out_shape).astype(jnp.bfloat16),
        first * factor,
        bias_sum * factor,
        second * factor,
    )


def solution(mesh):
    placed = (
        P("dp", "cp", None),
        P("dp", "cp", None),
        P("dp", "cp", None),
        P("dp", "cp", None),
        P("dp", "cp", None),
        P("dp", "cp", None),
        P("dp", None),
        P(),
        P(),
        P(),
    )
    plan = by_heads if mesh.shape["cp"] == 2 * GROUP_MOST else on_device
    return jax.shard_map(
        plan,
        mesh=mesh,
        in_specs=placed,
        out_specs=(P("dp", "cp", None), P("dp", "cp", None), P("dp", "cp", None), P(), P(), P()),
        check_vma=False,
    )
```

```python
import jax
import jax.numpy as jnp
from jax import lax
from jax.experimental import pallas as pl
from jax.experimental.pallas import tpu as pltpu
from jax.sharding import PartitionSpec as P

GROUP_MOST = 4


fire_floor = 64.0


def shifted_2(block, axis, distance):
    devices = range(lax.axis_size(axis))
    route = [(i - distance, i) for i in devices if i - distance in devices]
    return lax.ppermute(block, axis, route)


def shifted_3(shard, axis, by):
    count = lax.axis_size(axis)
    return lax.ppermute(shard, axis, [(i, (i + by) % count) for i in range(count)])


def seat_of(length_row, device):
    ends = jnp.cumsum(length_row)
    sequence = jnp.sum((ends <= device).astype(jnp.int32))
    before = jnp.sum(
        jnp.where(jnp.arange(length_row.shape[0], dtype=jnp.int32) < sequence, length_row, 0)
    )
    return (sequence, device - before)


def pair_terms(
    query_heads,
    grad_heads,
    log_block,
    delta_block,
    key_heads,
    value_heads,
    query_seq,
    query_pos,
    key_seq,
    key_pos,
    fire_w1,
    fire_b1,
    fire_w2,
):
    highest = lax.Precision.HIGHEST
    scale_value = query_heads.shape[2] ** (-0.5)
    allowed = (query_seq == key_seq) & (key_pos[None, :] <= query_pos[:, None])
    distance = jnp.maximum(query_pos[:, None] - key_pos[None, :], 0).astype(jnp.float32)
    denom = jnp.log1p(jnp.maximum(query_pos.astype(jnp.float32), fire_floor))
    ratio = jnp.log1p(distance) / denom[:, None]
    hidden_pre = fire_w1[:, None, None] * ratio[None] + fire_b1[:, None, None]
    hidden_act = jnp.maximum(hidden_pre, 0.0)
    pair_bias = jnp.einsum("cqk,ch->hqk", hidden_act, fire_w2, precision=highest)
    scores = (
        jnp.einsum("qhd,khd->hqk", query_heads, key_heads, preferred_element_type=jnp.float32)
        * scale_value
        + pair_bias
    )
    shifted = jnp.where(allowed[None], scores - log_block.T[:, :, None], -1e30)
    prob_block = jnp.exp(shifted)
    dprob = jnp.einsum("qhd,khd->hqk", grad_heads, value_heads, preferred_element_type=jnp.float32)
    dscore = prob_block * (dprob - delta_block.T[:, :, None])
    prob_low = prob_block.astype(jnp.bfloat16)
    score_low = dscore.astype(jnp.bfloat16)
    grad_query = (
        jnp.einsum("hqk,khd->qhd", score_low, key_heads, preferred_element_type=jnp.float32)
        * scale_value
    )
    grad_key = (
        jnp.einsum("hqk,qhd->khd", score_low, query_heads, preferred_element_type=jnp.float32)
        * scale_value
    )
    grad_value = jnp.einsum(
        "hqk,qhd->khd", prob_low, grad_heads, preferred_element_type=jnp.float32
    )
    grad_second = jnp.einsum("hqk,cqk->ch", dscore, hidden_act, precision=highest)
    grad_act = jnp.einsum("hqk,ch->cqk", dscore, fire_w2, precision=highest)
    grad_pre = jnp.where(hidden_pre > 0, grad_act, 0.0)
    grad_first = jnp.sum(grad_pre * ratio[None], axis=(1, 2))
    grad_bias = jnp.sum(grad_pre, axis=(1, 2))
    return (grad_query, grad_key, grad_value, grad_first, grad_bias, grad_second)


def rotate_keys(key_value):
    return shifted_2(key_value, "cp", 1)


MESH = pl.DeviceIdType.MESH
NT = (((1,), (1,)), ((), ()))
NN = (((1,), (0,)), ((), ()))
TN = (((0,), (0,)), ((), ()))
MASKED = -1e30
VMEM_BYTES = 62 * 2**20
BIAS_ROWS = 32
SUM_ROWS = 64


def exchange_kernel(
    q_ref,
    k_ref,
    v_ref,
    g_ref,
    o_ref,
    log_ref,
    lengths_ref,
    w1_ref,
    b1_ref,
    w2_ref,
    dq_ref,
    dk_ref,
    dv_ref,
    second_ref,
    lines_ref,
    held,
    own_g,
    own_o,
    stats,
    pair,
    ratios,
    grads,
    acc,
    coefs,
    cp_slots,
    dp_slots,
    own_sem,
    delta_sem,
    send_in,
    recv_in,
    send_stat,
    recv_stat,
    send_out,
    recv_out,
    send_cp,
    recv_cp,
    send_dp,
    recv_dp,
):
    parts = GROUP_MOST
    heads, tokens, size = held.shape[1:]
    rows = tokens // parts
    hidden = w1_ref.shape[0]
    heads_count = heads * parts
    delta_at = stats.shape[1] // 2
    cp_count, dp_count = cp_slots.shape[0], dp_slots.shape[0]
    scale_value = size ** (-0.5)
    me = lax.axis_index("cp")
    my_dp = lax.axis_index("dp")
    rank = lax.rem(me, parts)
    base = me - rank
    inputs = (q_ref, k_ref, v_ref, g_ref)
    results = (dq_ref, dk_ref, dv_ref)

    def dot(a, b, dims):
        return lax.dot_general(a, b, dims, preferred_element_type=jnp.float32)

    def peer_of(step):
        return lax.rem(rank + step, parts)

    def row_block(index):
        return pl.ds(pl.multiple_of(index * rows, rows), rows)

    def head_columns(part, head):
        return pl.ds(pl.multiple_of((part * heads + head) * size, size), size)

    def stat_copy(step):
        return pltpu.make_async_remote_copy(
            src_ref=stats.at[rank],
            dst_ref=stats.at[rank],
            send_sem=send_stat.at[step - 1],
            recv_sem=recv_stat.at[step - 1],
            device_id={"cp": base + peer_of(step)},
            device_id_type=MESH,
        )

    def in_copy(array, head, step):
        peer = peer_of(step)
        return pltpu.make_async_remote_copy(
            src_ref=inputs[array].at[:, head_columns(peer, head)],
            dst_ref=held.at[array, head, row_block(rank), :],
            send_sem=send_in.at[array, head, step - 1],
            recv_sem=recv_in.at[array, head, step - 1],
            device_id={"cp": base + peer},
            device_id_type=MESH,
        )

    def own_copy(array, head):
        return pltpu.make_async_copy(
            inputs[array].at[:, head_columns(rank, head)],
            held.at[array, head, row_block(rank), :],
            own_sem.at[array, head],
        )

    def out_copy(array, head, step):
        peer = peer_of(step)
        return pltpu.make_async_remote_copy(
            src_ref=grads.at[array, head, row_block(peer), :],
            dst_ref=results[array].at[:, head_columns(rank, head)],
            send_sem=send_out.at[array, head, step - 1],
            recv_sem=recv_out.at[array, head, step - 1],
            device_id={"cp": base + peer},
            device_id_type=MESH,
        )

    def cp_copy(step):
        return pltpu.make_async_remote_copy(
            src_ref=cp_slots.at[me],
            dst_ref=cp_slots.at[me],
            send_sem=send_cp.at[step - 1],
            recv_sem=recv_cp.at[step - 1],
            device_id={"cp": lax.rem(me + step, cp_count)},
            device_id_type=MESH,
        )

    def dp_copy(step):
        return pltpu.make_async_remote_copy(
            src_ref=dp_slots.at[my_dp],
            dst_ref=dp_slots.at[my_dp],
            send_sem=send_dp.at[step - 1],
            recv_sem=recv_dp.at[step - 1],
            device_id={"dp": lax.rem(my_dp + step, dp_count)},
            device_id_type=MESH,
        )

    delta_copies = (
        pltpu.make_async_copy(g_ref, own_g, delta_sem.at[0]),
        pltpu.make_async_copy(o_ref, own_o, delta_sem.at[1]),
    )
    for copy in delta_copies:
        copy.start()

    barrier = pltpu.get_barrier_semaphore()
    for step in range(1, cp_count):
        pl.semaphore_signal(
            barrier, inc=1, device_id={"cp": lax.rem(me + step, cp_count)}, device_id_type=MESH
        )
    for step in range(1, dp_count):
        pl.semaphore_signal(
            barrier, inc=1, device_id={"dp": lax.rem(my_dp + step, dp_count)}, device_id_type=MESH
        )
    pl.semaphore_wait(barrier, cp_count + dp_count - 2)

    def send_head(head, carry):
        for step in (2, 1, 3):
            for array in range(4):
                in_copy(array, head, step).start()
        for array in range(4):
            own_copy(array, head).start()
        return carry

    early = 2
    lax.fori_loop(0, early, send_head, 0)

    stats[rank] = jnp.zeros(stats.shape[1:], jnp.float32)
    stats[rank, 0:heads_count, :] = log_ref[:, 0, :]
    for copy in delta_copies:
        copy.wait()
    ones = jnp.ones((8, 2 * size), jnp.bfloat16)

    def delta_head(head, carry):
        columns = pl.ds(pl.multiple_of(head * size, size), size)
        product = own_g[:, columns].astype(jnp.float32) * own_o[:, columns].astype(jnp.float32)
        high = product.astype(jnp.bfloat16)
        rest = (product - high.astype(jnp.float32)).astype(jnp.bfloat16)
        row = dot(ones, jnp.concatenate([high, rest], axis=1), NT)
        stats[rank, pl.ds(delta_at + head, 1), :] = row[0:1]
        return carry

    lax.fori_loop(0, heads_count, delta_head, 0)
    for step in range(1, parts):
        stat_copy(step).start()
    lax.fori_loop(early, heads, send_head, 0)

    def bias_column(block, carry):
        columns = row_block(block)
        start = jnp.int32(0)
        end = jnp.int32(0)
        for index in range(lengths_ref.shape[1]):
            start = jnp.where(end <= base + block, end, start)
            end = end + lengths_ref[0, index]
        start = (start - base) * rows
        query_row = block * rows + lax.broadcasted_iota(jnp.int32, (1, rows), 1)
        position = (query_row - start).astype(jnp.float32)
        rden = 1.0 / jnp.log(1.0 + jnp.maximum(position, fire_floor))

        def bias_rows(chunk, carry):
            at = pl.ds(pl.multiple_of(chunk * BIAS_ROWS, BIAS_ROWS), BIAS_ROWS)
            key_at = chunk * BIAS_ROWS + lax.broadcasted_iota(jnp.int32, (BIAS_ROWS, rows), 0)
            query_at = block * rows + lax.broadcasted_iota(jnp.int32, (BIAS_ROWS, rows), 1)
            allowed = (key_at >= start) & (key_at <= query_at)
            distance = jnp.maximum(query_at - key_at, 0).astype(jnp.float32)
            ratio = jnp.log(1.0 + distance) * rden
            ratios[at, columns] = ratio
            totals = [jnp.zeros((BIAS_ROWS, rows), jnp.float32) for _ in range(heads)]
            for unit in range(hidden):
                act = jnp.maximum(ratio * w1_ref[unit] + b1_ref[unit], 0.0)
                for head in range(heads):
                    totals[head] = totals[head] + act * w2_ref[rank * heads + head, unit]
            for head in range(heads):
                pair[head, at, columns] = jnp.where(allowed, totals[head], MASKED)
            return carry

        return lax.fori_loop(0, (block + 1) * (rows // BIAS_ROWS), bias_rows, carry)

    lax.fori_loop(0, parts, bias_column, 0)
    half = 2 * rows
    for head in range(heads):
        for first in range(0, parts, 2):
            pair[head, (first + 1) * rows : (first + 2) * rows, first * rows : (first + 1) * rows] = (
                jnp.full((rows, rows), MASKED, jnp.float32)
            )
    acc[...] = jnp.zeros_like(acc)
    unit_at = lax.broadcasted_iota(jnp.int32, (hidden, 128), 0)
    lane_at = lax.broadcasted_iota(jnp.int32, (hidden, 128), 1)
    coef = jnp.zeros((hidden, 128), jnp.float32)
    for unit in range(hidden):
        line = jnp.where(lane_at == 0, w1_ref[unit], b1_ref[unit])
        for head in range(heads):
            line = jnp.where(lane_at == 2 + head, w2_ref[rank * heads + head, unit], line)
        coef = jnp.where(unit_at == unit, line, coef)
    coefs[...] = coef

    for step in range(1, parts):
        stat_copy(step).wait_recv()

    def one_head(head, carry):
        for array in range(4):
            own_copy(array, head).wait()
        for step in (2, 1, 3):
            for array in range(4):
                in_copy(array, head, step).wait_recv()
        at = rank * heads + head
        log_row = jnp.concatenate([stats[part, pl.ds(at, 1), :] for part in range(parts)], axis=1)
        delta_row = jnp.concatenate(
            [stats[part, pl.ds(delta_at + at, 1), :] for part in range(parts)], axis=1
        )

        dq = [None, None]
        dk = [None, None]
        dv = [None, None]

        def plus(total, term):
            return term if total is None else total + term

        for kt, qt in ((0, 0), (0, 1), (1, 1)):
            krows = slice(kt * half, (kt + 1) * half)
            qrows = slice(qt * half, (qt + 1) * half)
            q = held[0, head, qrows, :]
            k = held[1, head, krows, :]
            v = held[2, head, krows, :]
            g = held[3, head, qrows, :]
            scores = dot(k, q, NT) * scale_value + pair[head, krows, qrows]
            prob = jnp.exp(scores - log_row[:, qrows])
            dscore = prob * (dot(v, g, NT) - delta_row[:, qrows])
            pair[head, krows, qrows] = dscore
            prob_low = prob.astype(jnp.bfloat16)
            score_low = dscore.astype(jnp.bfloat16)
            dv[kt] = plus(dv[kt], dot(prob_low, g, NN))
            dk[kt] = plus(dk[kt], dot(score_low, q, NN))
            dq[qt] = plus(dq[qt], dot(score_low, k, TN))
        for tile in range(2):
            trows = slice(tile * half, (tile + 1) * half)
            grads[0, head, trows, :] = (dq[tile] * scale_value).astype(jnp.bfloat16)
            grads[1, head, trows, :] = (dk[tile] * scale_value).astype(jnp.bfloat16)
            grads[2, head, trows, :] = dv[tile].astype(jnp.bfloat16)
        for step in (2, 1, 3):
            for array in range(3):
                out_copy(array, head, step).start()
        for array in range(3):
            results[array][:, head_columns(rank, head)] = grads[array, head, row_block(rank), :]
        return carry

    lax.fori_loop(0, heads, one_head, 0)

    def sum_column(block, carry):
        columns = row_block(block)

        def sum_rows(chunk, carry):
            at = pl.ds(pl.multiple_of(chunk * SUM_ROWS, SUM_ROWS), SUM_ROWS)
            ratio = ratios[at, columns]
            flat = [pair[head, at, columns] for head in range(heads)]
            lives, terms = [], []
            for row in range(0, SUM_ROWS, 8):
                part = ratio[row : row + 8]
                live = [
                    jnp.where(part * w1_ref[unit] > -b1_ref[unit], 1.0, 0.0)
                    for unit in range(hidden)
                ]
                lives.append(jnp.concatenate(live, axis=0).astype(jnp.bfloat16))
                term = [flat[head][row : row + 8] for head in range(heads)]
                term = jnp.concatenate(term + [one * part for one in term], axis=0)
                high = term.astype(jnp.bfloat16)
                rest = (term - high.astype(jnp.float32)).astype(jnp.bfloat16)
                terms.append(jnp.concatenate([high, rest], axis=0))
            acc[...] += dot(
                jnp.concatenate(lives, axis=1), jnp.concatenate(terms, axis=1), NT
            )
            return carry

        return lax.fori_loop(0, (block + 1) * (rows // SUM_ROWS), sum_rows, carry)

    lax.fori_loop(0, parts, sum_column, 0)

    across = acc.shape[1]
    same = lax.rem(lax.broadcasted_iota(jnp.int32, acc.shape, 0), 8) == lax.rem(
        lax.broadcasted_iota(jnp.int32, acc.shape, 1), 8
    )
    folded = jnp.sum(jnp.where(same, acc[...], 0.0).reshape(hidden, 8, across), axis=1)
    kind = lax.rem(lax.broadcasted_iota(jnp.int32, (hidden, across), 1) // 8, 2 * heads)
    lane = lax.broadcasted_iota(jnp.int32, (hidden, 128), 1)
    message = jnp.zeros((hidden, 128), jnp.float32)
    first = jnp.zeros((hidden, 1), jnp.float32)
    bias_sum = jnp.zeros((hidden, 1), jnp.float32)
    w1_column, b1_column = coefs[:, 0:1], coefs[:, 1:2]
    for head in range(heads):
        flat = jnp.sum(jnp.where(kind == head, folded, 0.0), axis=1, keepdims=True)
        tilted = jnp.sum(jnp.where(kind == heads + head, folded, 0.0), axis=1, keepdims=True)
        weight = coefs[:, 2 + head : 3 + head]
        first = first + tilted * weight
        bias_sum = bias_sum + flat * weight
        second = tilted * w1_column + flat * b1_column
        message = jnp.where(lane == rank * heads + head, second, message)
    message = jnp.where(lane == heads_count, first, message)
    message = jnp.where(lane == heads_count + 1, bias_sum, message)
    cp_slots[me] = message
    for step in range(1, cp_count):
        cp_copy(step).start()
    for step in range(1, cp_count):
        cp_copy(step).wait()
    total = cp_slots[0]
    for index in range(1, cp_count):
        total = total + cp_slots[index]
    dp_slots[my_dp] = total
    for step in range(1, dp_count):
        dp_copy(step).start()
    for step in range(1, dp_count):
        dp_copy(step).wait()
    total = dp_slots[0]
    for index in range(1, dp_count):
        total = total + dp_slots[index]
    total = (total * (dp_count * cp_count * rows) ** (-0.5)).T
    second_ref[...] = total[0:heads_count]
    lines_ref[...] = total[heads_count : heads_count + 2]

    def drain_head(head, carry):
        for step in (2, 1, 3):
            for array in range(4):
                in_copy(array, head, step).wait_send()
            for array in range(3):
                out_copy(array, head, step).wait()
        return carry

    lax.fori_loop(0, heads, drain_head, 0)
    for step in range(1, parts):
        stat_copy(step).wait_send()


def by_heads(queries, keys, values, outputs, d_out, log_norm, lengths, fire_w1, fire_b1, fire_w2):
    rows_dev = queries.shape[1]
    heads_count = log_norm.shape[2]
    feature_count = queries.shape[2]
    head_size = feature_count // heads_count
    cp_count, dp_count = lax.axis_size("cp"), lax.axis_size("dp")
    parts = GROUP_MOST
    heads = heads_count // parts
    hidden = fire_w1.shape[0]
    tokens = parts * rows_dev
    stat_rows = 2 * (-(-heads_count // 8) * 8)

    hbm = pl.BlockSpec(memory_space=pltpu.HBM)
    vmem = pl.BlockSpec(memory_space=pltpu.VMEM)
    smem = pl.BlockSpec(memory_space=pltpu.SMEM)
    low = jnp.bfloat16
    wide = jnp.float32
    block = jax.ShapeDtypeStruct((rows_dev, feature_count), low)
    steps = parts - 1
    dma = pltpu.SemaphoreType.DMA
    grad_q, grad_k, grad_v, second, lines = pl.pallas_call(
        exchange_kernel,
        out_shape=(
            block,
            block,
            block,
            jax.ShapeDtypeStruct((heads_count, hidden), wide),
            jax.ShapeDtypeStruct((2, hidden), wide),
        ),
        in_specs=[hbm] * 5 + [vmem] + [smem] * 4,
        out_specs=(vmem,) * 5,
        scratch_shapes=[
            pltpu.VMEM((4, heads, tokens, head_size), low),
            pltpu.VMEM((rows_dev, feature_count), low),
            pltpu.VMEM((rows_dev, feature_count), low),
            pltpu.VMEM((parts, stat_rows, rows_dev), wide),
            pltpu.VMEM((heads, tokens, tokens), wide),
            pltpu.VMEM((tokens, tokens), wide),
            pltpu.VMEM((3, heads, tokens, head_size), low),
            pltpu.VMEM((hidden * 8, 4 * heads * 8), wide),
            pltpu.VMEM((hidden, 128), wide),
            pltpu.VMEM((cp_count, hidden, 128), wide),
            pltpu.VMEM((dp_count, hidden, 128), wide),
            dma((4, heads)),
            dma((2,)),
            dma((4, heads, steps)),
            dma((4, heads, steps)),
            dma((steps,)),
            dma((steps,)),
            dma((3, heads, steps)),
            dma((3, heads, steps)),
            dma((cp_count - 1,)),
            dma((cp_count - 1,)),
            dma((dp_count - 1,)),
            dma((dp_count - 1,)),
        ],
        compiler_params=pltpu.CompilerParams(
            collective_id=0, has_side_effects=True, vmem_limit_bytes=VMEM_BYTES
        ),
    )(
        queries[0],
        keys[0],
        values[0],
        d_out[0],
        outputs[0],
        log_norm.transpose(2, 0, 1),
        lengths,
        fire_w1,
        fire_b1,
        fire_w2.T,
    )
    return (
        grad_q[None],
        grad_k[None],
        grad_v[None],
        lines[0],
        lines[1],
        second.T,
    )


def on_device(queries, keys, values, outputs, d_out, log_norm, lengths, fire_w1, fire_b1, fire_w2):
    rows_dev = queries.shape[1]
    heads_count = log_norm.shape[2]
    feature_count = queries.shape[2]
    head_size = feature_count // heads_count
    cp_count = lax.axis_size("cp")
    my_index = lax.axis_index("cp")
    length_row = lengths[0]
    reach = GROUP_MOST - 1
    query_heads = queries[0].reshape(rows_dev, heads_count, head_size)
    key_heads = keys[0].reshape(rows_dev, heads_count, head_size)
    value_heads = values[0].reshape(rows_dev, heads_count, head_size)
    grad_heads = d_out[0].reshape(rows_dev, heads_count, head_size)
    out_heads = outputs[0].reshape(rows_dev, heads_count, head_size)
    log_block = log_norm[0]
    delta_block = jnp.einsum(
        "qhd,qhd->qh", grad_heads, out_heads, preferred_element_type=jnp.float32
    )
    token_index = jnp.arange(rows_dev, dtype=jnp.int32)

    def seat_positions(device):
        sequence, offset = seat_of(length_row, device)
        return (sequence, offset * rows_dev + token_index)

    my_seq, my_pos = seat_positions(my_index)
    local = pair_terms(
        query_heads,
        grad_heads,
        log_block,
        delta_block,
        key_heads,
        value_heads,
        my_seq,
        my_pos,
        my_seq,
        my_pos,
        fire_w1,
        fire_b1,
        fire_w2,
    )
    key_value = jnp.stack([key_heads, value_heads])

    def carried_hop(hop_index, carry):
        moving_kv, moving_grads, grad_q, first, bias_sum, second = carry
        moving_kv = rotate_keys(moving_kv)
        moving_grads = shifted_3(moving_grads, "cp", 1)
        key_seq, key_pos = seat_positions((my_index - hop_index) % cp_count)
        terms = pair_terms(
            query_heads,
            grad_heads,
            log_block,
            delta_block,
            moving_kv[0],
            moving_kv[1],
            my_seq,
            my_pos,
            key_seq,
            key_pos,
            fire_w1,
            fire_b1,
            fire_w2,
        )
        moving_grads = moving_grads + jnp.stack([terms[1], terms[2]])
        return (
            moving_kv,
            moving_grads,
            grad_q + terms[0],
            first + terms[3],
            bias_sum + terms[4],
            second + terms[5],
        )

    start = (key_value, jnp.stack([local[1], local[2]]), local[0], local[3], local[4], local[5])
    result = lax.fori_loop(1, GROUP_MOST, carried_hop, start)
    grad_q, first, bias_sum, second = (result[2], result[3], result[4], result[5])
    home_grads = shifted_3(result[1].astype(jnp.bfloat16), "cp", -reach).astype(jnp.float32)
    grad_k, grad_v = (home_grads[0], home_grads[1])
    first, bias_sum, second = lax.psum((first, bias_sum, second), ("cp", "dp"))
    factor = (lax.axis_size("dp") * cp_count * rows_dev) ** (-0.5)
    out_shape = (1, rows_dev, feature_count)
    return (
        grad_q.reshape(out_shape).astype(jnp.bfloat16),
        grad_k.reshape(out_shape).astype(jnp.bfloat16),
        grad_v.reshape(out_shape).astype(jnp.bfloat16),
        first * factor,
        bias_sum * factor,
        second * factor,
    )


def solution(mesh):
    placed = (
        P("dp", "cp", None),
        P("dp", "cp", None),
        P("dp", "cp", None),
        P("dp", "cp", None),
        P("dp", "cp", None),
        P("dp", "cp", None),
        P("dp", None),
        P(),
        P(),
        P(),
    )
    plan = by_heads if mesh.shape["cp"] == 2 * GROUP_MOST else on_device
    return jax.shard_map(
        plan,
        mesh=mesh,
        in_specs=placed,
        out_specs=(P("dp", "cp", None), P("dp", "cp", None), P("dp", "cp", None), P(), P(), P()),
        check_vma=False,
    )
```

```python
import jax
import jax.numpy as jnp
from jax import lax
from jax.experimental import pallas as pl
from jax.experimental.pallas import tpu as pltpu
from jax.sharding import PartitionSpec as P

GROUP_MOST = 4


fire_floor = 64.0


def shifted_2(block, axis, distance):
    devices = range(lax.axis_size(axis))
    route = [(i - distance, i) for i in devices if i - distance in devices]
    return lax.ppermute(block, axis, route)


def shifted_3(shard, axis, by):
    count = lax.axis_size(axis)
    return lax.ppermute(shard, axis, [(i, (i + by) % count) for i in range(count)])


def seat_of(length_row, device):
    ends = jnp.cumsum(length_row)
    sequence = jnp.sum((ends <= device).astype(jnp.int32))
    before = jnp.sum(
        jnp.where(jnp.arange(length_row.shape[0], dtype=jnp.int32) < sequence, length_row, 0)
    )
    return (sequence, device - before)


def pair_terms(
    query_heads,
    grad_heads,
    log_block,
    delta_block,
    key_heads,
    value_heads,
    query_seq,
    query_pos,
    key_seq,
    key_pos,
    fire_w1,
    fire_b1,
    fire_w2,
):
    highest = lax.Precision.HIGHEST
    scale_value = query_heads.shape[2] ** (-0.5)
    allowed = (query_seq == key_seq) & (key_pos[None, :] <= query_pos[:, None])
    distance = jnp.maximum(query_pos[:, None] - key_pos[None, :], 0).astype(jnp.float32)
    denom = jnp.log1p(jnp.maximum(query_pos.astype(jnp.float32), fire_floor))
    ratio = jnp.log1p(distance) / denom[:, None]
    hidden_pre = fire_w1[:, None, None] * ratio[None] + fire_b1[:, None, None]
    hidden_act = jnp.maximum(hidden_pre, 0.0)
    pair_bias = jnp.einsum("cqk,ch->hqk", hidden_act, fire_w2, precision=highest)
    scores = (
        jnp.einsum("qhd,khd->hqk", query_heads, key_heads, preferred_element_type=jnp.float32)
        * scale_value
        + pair_bias
    )
    shifted = jnp.where(allowed[None], scores - log_block.T[:, :, None], -1e30)
    prob_block = jnp.exp(shifted)
    dprob = jnp.einsum("qhd,khd->hqk", grad_heads, value_heads, preferred_element_type=jnp.float32)
    dscore = prob_block * (dprob - delta_block.T[:, :, None])
    prob_low = prob_block.astype(jnp.bfloat16)
    score_low = dscore.astype(jnp.bfloat16)
    grad_query = (
        jnp.einsum("hqk,khd->qhd", score_low, key_heads, preferred_element_type=jnp.float32)
        * scale_value
    )
    grad_key = (
        jnp.einsum("hqk,qhd->khd", score_low, query_heads, preferred_element_type=jnp.float32)
        * scale_value
    )
    grad_value = jnp.einsum(
        "hqk,qhd->khd", prob_low, grad_heads, preferred_element_type=jnp.float32
    )
    grad_second = jnp.einsum("hqk,cqk->ch", dscore, hidden_act, precision=highest)
    grad_act = jnp.einsum("hqk,ch->cqk", dscore, fire_w2, precision=highest)
    grad_pre = jnp.where(hidden_pre > 0, grad_act, 0.0)
    grad_first = jnp.sum(grad_pre * ratio[None], axis=(1, 2))
    grad_bias = jnp.sum(grad_pre, axis=(1, 2))
    return (grad_query, grad_key, grad_value, grad_first, grad_bias, grad_second)


def rotate_keys(key_value):
    return shifted_2(key_value, "cp", 1)


MESH = pl.DeviceIdType.MESH
NT = (((1,), (1,)), ((), ()))
NN = (((1,), (0,)), ((), ()))
TN = (((0,), (0,)), ((), ()))
MASKED = -1e30
VMEM_BYTES = 62 * 2**20
BIAS_ROWS = 32
SUM_ROWS = 64


def exchange_kernel(
    q_ref,
    k_ref,
    v_ref,
    g_ref,
    o_ref,
    log_ref,
    lengths_ref,
    w1_ref,
    b1_ref,
    w2_ref,
    dq_ref,
    dk_ref,
    dv_ref,
    second_ref,
    lines_ref,
    held,
    own_g,
    own_o,
    stats,
    pair,
    ratios,
    grads,
    acc,
    coefs,
    cp_slots,
    dp_slots,
    own_sem,
    delta_sem,
    send_in,
    recv_in,
    send_stat,
    recv_stat,
    send_out,
    recv_out,
    send_cp,
    recv_cp,
    send_dp,
    recv_dp,
):
    parts = GROUP_MOST
    heads, tokens, size = held.shape[1:]
    rows = tokens // parts
    hidden = w1_ref.shape[0]
    heads_count = heads * parts
    delta_at = stats.shape[1] // 2
    cp_count, dp_count = cp_slots.shape[0], dp_slots.shape[0]
    scale_value = size ** (-0.5)
    me = lax.axis_index("cp")
    my_dp = lax.axis_index("dp")
    rank = lax.rem(me, parts)
    base = me - rank
    inputs = (q_ref, k_ref, v_ref, g_ref)
    results = (dq_ref, dk_ref, dv_ref)

    def dot(a, b, dims):
        return lax.dot_general(a, b, dims, preferred_element_type=jnp.float32)

    def peer_of(step):
        return lax.rem(rank + step, parts)

    def row_block(index):
        return pl.ds(pl.multiple_of(index * rows, rows), rows)

    def head_columns(part, head):
        return pl.ds(pl.multiple_of((part * heads + head) * size, size), size)

    def stat_copy(step):
        return pltpu.make_async_remote_copy(
            src_ref=stats.at[rank],
            dst_ref=stats.at[rank],
            send_sem=send_stat.at[step - 1],
            recv_sem=recv_stat.at[step - 1],
            device_id={"cp": base + peer_of(step)},
            device_id_type=MESH,
        )

    def in_copy(array, head, step):
        peer = peer_of(step)
        return pltpu.make_async_remote_copy(
            src_ref=inputs[array].at[:, head_columns(peer, head)],
            dst_ref=held.at[array, head, row_block(rank), :],
            send_sem=send_in.at[array, head, step - 1],
            recv_sem=recv_in.at[array, head, step - 1],
            device_id={"cp": base + peer},
            device_id_type=MESH,
        )

    def own_copy(array, head):
        return pltpu.make_async_copy(
            inputs[array].at[:, head_columns(rank, head)],
            held.at[array, head, row_block(rank), :],
            own_sem.at[array, head],
        )

    def out_copy(array, head, step):
        peer = peer_of(step)
        return pltpu.make_async_remote_copy(
            src_ref=grads.at[array, head, row_block(peer), :],
            dst_ref=results[array].at[:, head_columns(rank, head)],
            send_sem=send_out.at[array, head, step - 1],
            recv_sem=recv_out.at[array, head, step - 1],
            device_id={"cp": base + peer},
            device_id_type=MESH,
        )

    def cp_copy(step):
        return pltpu.make_async_remote_copy(
            src_ref=cp_slots.at[me],
            dst_ref=cp_slots.at[me],
            send_sem=send_cp.at[step - 1],
            recv_sem=recv_cp.at[step - 1],
            device_id={"cp": lax.rem(me + step, cp_count)},
            device_id_type=MESH,
        )

    def dp_copy(step):
        return pltpu.make_async_remote_copy(
            src_ref=dp_slots.at[my_dp],
            dst_ref=dp_slots.at[my_dp],
            send_sem=send_dp.at[step - 1],
            recv_sem=recv_dp.at[step - 1],
            device_id={"dp": lax.rem(my_dp + step, dp_count)},
            device_id_type=MESH,
        )

    delta_copies = (
        pltpu.make_async_copy(g_ref, own_g, delta_sem.at[0]),
        pltpu.make_async_copy(o_ref, own_o, delta_sem.at[1]),
    )
    for copy in delta_copies:
        copy.start()

    barrier = pltpu.get_barrier_semaphore()
    for step in range(1, cp_count):
        pl.semaphore_signal(
            barrier, inc=1, device_id={"cp": lax.rem(me + step, cp_count)}, device_id_type=MESH
        )
    for step in range(1, dp_count):
        pl.semaphore_signal(
            barrier, inc=1, device_id={"dp": lax.rem(my_dp + step, dp_count)}, device_id_type=MESH
        )
    pl.semaphore_wait(barrier, cp_count + dp_count - 2)

    def send_head(head, carry):
        for step in (2, 1, 3):
            for array in range(4):
                in_copy(array, head, step).start()
        for array in range(4):
            own_copy(array, head).start()
        return carry

    early = 2
    lax.fori_loop(0, early, send_head, 0)

    stats[rank] = jnp.zeros(stats.shape[1:], jnp.float32)
    stats[rank, 0:heads_count, :] = log_ref[:, 0, :]
    for copy in delta_copies:
        copy.wait()
    ones = jnp.ones((8, 2 * size), jnp.bfloat16)

    def delta_head(head, carry):
        columns = pl.ds(pl.multiple_of(head * size, size), size)
        product = own_g[:, columns].astype(jnp.float32) * own_o[:, columns].astype(jnp.float32)
        high = product.astype(jnp.bfloat16)
        rest = (product - high.astype(jnp.float32)).astype(jnp.bfloat16)
        row = dot(ones, jnp.concatenate([high, rest], axis=1), NT)
        stats[rank, pl.ds(delta_at + head, 1), :] = row[0:1]
        return carry

    lax.fori_loop(0, heads_count, delta_head, 0)
    for step in range(1, parts):
        stat_copy(step).start()
    lax.fori_loop(early, heads, send_head, 0)

    def bias_column(block, carry):
        columns = row_block(block)
        start = jnp.int32(0)
        end = jnp.int32(0)
        for index in range(lengths_ref.shape[1]):
            start = jnp.where(end <= base + block, end, start)
            end = end + lengths_ref[0, index]
        start = (start - base) * rows
        query_row = block * rows + lax.broadcasted_iota(jnp.int32, (1, rows), 1)
        position = (query_row - start).astype(jnp.float32)
        rden = 1.0 / jnp.log(1.0 + jnp.maximum(position, fire_floor))

        def bias_rows(chunk, carry):
            at = pl.ds(pl.multiple_of(chunk * BIAS_ROWS, BIAS_ROWS), BIAS_ROWS)
            key_at = chunk * BIAS_ROWS + lax.broadcasted_iota(jnp.int32, (BIAS_ROWS, rows), 0)
            query_at = block * rows + lax.broadcasted_iota(jnp.int32, (BIAS_ROWS, rows), 1)
            allowed = (key_at >= start) & (key_at <= query_at)
            distance = jnp.maximum(query_at - key_at, 0).astype(jnp.float32)
            ratio = jnp.log(1.0 + distance) * rden
            ratios[at, columns] = ratio
            totals = [jnp.zeros((BIAS_ROWS, rows), jnp.float32) for _ in range(heads)]
            for unit in range(hidden):
                act = jnp.maximum(ratio * w1_ref[unit] + b1_ref[unit], 0.0)
                for head in range(heads):
                    totals[head] = totals[head] + act * w2_ref[rank * heads + head, unit]
            for head in range(heads):
                pair[head, at, columns] = jnp.where(allowed, totals[head], MASKED)
            return carry

        return lax.fori_loop(0, (block + 1) * (rows // BIAS_ROWS), bias_rows, carry)

    lax.fori_loop(0, parts, bias_column, 0)
    half = 2 * rows
    for head in range(heads):
        for first in range(0, parts, 2):
            pair[head, (first + 1) * rows : (first + 2) * rows, first * rows : (first + 1) * rows] = (
                jnp.full((rows, rows), MASKED, jnp.float32)
            )
    acc[...] = jnp.zeros_like(acc)
    unit_at = lax.broadcasted_iota(jnp.int32, (hidden, 128), 0)
    lane_at = lax.broadcasted_iota(jnp.int32, (hidden, 128), 1)
    coef = jnp.zeros((hidden, 128), jnp.float32)
    for unit in range(hidden):
        line = jnp.where(lane_at == 0, w1_ref[unit], b1_ref[unit])
        for head in range(heads):
            line = jnp.where(lane_at == 2 + head, w2_ref[rank * heads + head, unit], line)
        coef = jnp.where(unit_at == unit, line, coef)
    coefs[...] = coef

    for step in range(1, parts):
        stat_copy(step).wait_recv()

    def one_head(head, carry):
        for array in range(4):
            own_copy(array, head).wait()
        for step in (2, 1, 3):
            for array in range(4):
                in_copy(array, head, step).wait_recv()
        at = rank * heads + head
        log_row = jnp.concatenate([stats[part, pl.ds(at, 1), :] for part in range(parts)], axis=1)
        delta_row = jnp.concatenate(
            [stats[part, pl.ds(delta_at + at, 1), :] for part in range(parts)], axis=1
        )

        dq = [None, None]
        dk = [None, None]
        dv = [None, None]

        def plus(total, term):
            return term if total is None else total + term

        for kt, qt in ((0, 0), (0, 1), (1, 1)):
            krows = slice(kt * half, (kt + 1) * half)
            qrows = slice(qt * half, (qt + 1) * half)
            q = held[0, head, qrows, :]
            k = held[1, head, krows, :]
            v = held[2, head, krows, :]
            g = held[3, head, qrows, :]
            scores = dot(k, q, NT) * scale_value + pair[head, krows, qrows]
            prob = jnp.exp(scores - log_row[:, qrows])
            dscore = prob * (dot(v, g, NT) - delta_row[:, qrows])
            pair[head, krows, qrows] = dscore
            prob_low = prob.astype(jnp.bfloat16)
            score_low = dscore.astype(jnp.bfloat16)
            dv[kt] = plus(dv[kt], dot(prob_low, g, NN))
            dk[kt] = plus(dk[kt], dot(score_low, q, NN))
            dq[qt] = plus(dq[qt], dot(score_low, k, TN))
        for tile in range(2):
            trows = slice(tile * half, (tile + 1) * half)
            grads[0, head, trows, :] = (dq[tile] * scale_value).astype(jnp.bfloat16)
            grads[1, head, trows, :] = (dk[tile] * scale_value).astype(jnp.bfloat16)
            grads[2, head, trows, :] = dv[tile].astype(jnp.bfloat16)
        for array in range(3):
            results[array][:, head_columns(rank, head)] = grads[array, head, row_block(rank), :]
        return carry

    def return_head(head, carry):
        for step in (2, 1, 3):
            for array in range(3):
                out_copy(array, head, step).start()
        return carry

    prompt = heads - 2
    lax.fori_loop(0, prompt, lambda head, carry: return_head(head, one_head(head, carry)), 0)
    lax.fori_loop(prompt, heads, one_head, 0)

    def sum_column(block, carry):
        columns = row_block(block)

        def sum_rows(chunk, carry):
            at = pl.ds(pl.multiple_of(chunk * SUM_ROWS, SUM_ROWS), SUM_ROWS)
            ratio = ratios[at, columns]
            flat = [pair[head, at, columns] for head in range(heads)]
            lives, terms = [], []
            for row in range(0, SUM_ROWS, 8):
                part = ratio[row : row + 8]
                live = [
                    jnp.where(part * w1_ref[unit] > -b1_ref[unit], 1.0, 0.0)
                    for unit in range(hidden)
                ]
                lives.append(jnp.concatenate(live, axis=0).astype(jnp.bfloat16))
                term = [flat[head][row : row + 8] for head in range(heads)]
                term = jnp.concatenate(term + [one * part for one in term], axis=0)
                high = term.astype(jnp.bfloat16)
                rest = (term - high.astype(jnp.float32)).astype(jnp.bfloat16)
                terms.append(jnp.concatenate([high, rest], axis=0))
            acc[...] += dot(
                jnp.concatenate(lives, axis=1), jnp.concatenate(terms, axis=1), NT
            )
            return carry

        return lax.fori_loop(0, (block + 1) * (rows // SUM_ROWS), sum_rows, carry)

    lax.fori_loop(0, parts, sum_column, 0)

    across = acc.shape[1]
    same = lax.rem(lax.broadcasted_iota(jnp.int32, acc.shape, 0), 8) == lax.rem(
        lax.broadcasted_iota(jnp.int32, acc.shape, 1), 8
    )
    folded = jnp.sum(jnp.where(same, acc[...], 0.0).reshape(hidden, 8, across), axis=1)
    kind = lax.rem(lax.broadcasted_iota(jnp.int32, (hidden, across), 1) // 8, 2 * heads)
    lane = lax.broadcasted_iota(jnp.int32, (hidden, 128), 1)
    message = jnp.zeros((hidden, 128), jnp.float32)
    first = jnp.zeros((hidden, 1), jnp.float32)
    bias_sum = jnp.zeros((hidden, 1), jnp.float32)
    w1_column, b1_column = coefs[:, 0:1], coefs[:, 1:2]
    for head in range(heads):
        flat = jnp.sum(jnp.where(kind == head, folded, 0.0), axis=1, keepdims=True)
        tilted = jnp.sum(jnp.where(kind == heads + head, folded, 0.0), axis=1, keepdims=True)
        weight = coefs[:, 2 + head : 3 + head]
        first = first + tilted * weight
        bias_sum = bias_sum + flat * weight
        second = tilted * w1_column + flat * b1_column
        message = jnp.where(lane == rank * heads + head, second, message)
    message = jnp.where(lane == heads_count, first, message)
    message = jnp.where(lane == heads_count + 1, bias_sum, message)
    cp_slots[me] = message
    for step in range(1, cp_count):
        cp_copy(step).start()
    lax.fori_loop(prompt, heads, return_head, 0)
    for step in range(1, cp_count):
        cp_copy(step).wait()
    total = cp_slots[0]
    for index in range(1, cp_count):
        total = total + cp_slots[index]
    dp_slots[my_dp] = total
    for step in range(1, dp_count):
        dp_copy(step).start()
    for step in range(1, dp_count):
        dp_copy(step).wait()
    total = dp_slots[0]
    for index in range(1, dp_count):
        total = total + dp_slots[index]
    total = (total * (dp_count * cp_count * rows) ** (-0.5)).T
    second_ref[...] = total[0:heads_count]
    lines_ref[...] = total[heads_count : heads_count + 2]

    def drain_head(head, carry):
        for step in (2, 1, 3):
            for array in range(4):
                in_copy(array, head, step).wait_send()
            for array in range(3):
                out_copy(array, head, step).wait()
        return carry

    lax.fori_loop(0, heads, drain_head, 0)
    for step in range(1, parts):
        stat_copy(step).wait_send()


def by_heads(queries, keys, values, outputs, d_out, log_norm, lengths, fire_w1, fire_b1, fire_w2):
    rows_dev = queries.shape[1]
    heads_count = log_norm.shape[2]
    feature_count = queries.shape[2]
    head_size = feature_count // heads_count
    cp_count, dp_count = lax.axis_size("cp"), lax.axis_size("dp")
    parts = GROUP_MOST
    heads = heads_count // parts
    hidden = fire_w1.shape[0]
    tokens = parts * rows_dev
    stat_rows = 2 * (-(-heads_count // 8) * 8)

    hbm = pl.BlockSpec(memory_space=pltpu.HBM)
    vmem = pl.BlockSpec(memory_space=pltpu.VMEM)
    smem = pl.BlockSpec(memory_space=pltpu.SMEM)
    low = jnp.bfloat16
    wide = jnp.float32
    block = jax.ShapeDtypeStruct((rows_dev, feature_count), low)
    steps = parts - 1
    dma = pltpu.SemaphoreType.DMA
    grad_q, grad_k, grad_v, second, lines = pl.pallas_call(
        exchange_kernel,
        out_shape=(
            block,
            block,
            block,
            jax.ShapeDtypeStruct((heads_count, hidden), wide),
            jax.ShapeDtypeStruct((2, hidden), wide),
        ),
        in_specs=[hbm] * 5 + [vmem] + [smem] * 4,
        out_specs=(vmem,) * 5,
        scratch_shapes=[
            pltpu.VMEM((4, heads, tokens, head_size), low),
            pltpu.VMEM((rows_dev, feature_count), low),
            pltpu.VMEM((rows_dev, feature_count), low),
            pltpu.VMEM((parts, stat_rows, rows_dev), wide),
            pltpu.VMEM((heads, tokens, tokens), wide),
            pltpu.VMEM((tokens, tokens), wide),
            pltpu.VMEM((3, heads, tokens, head_size), low),
            pltpu.VMEM((hidden * 8, 4 * heads * 8), wide),
            pltpu.VMEM((hidden, 128), wide),
            pltpu.VMEM((cp_count, hidden, 128), wide),
            pltpu.VMEM((dp_count, hidden, 128), wide),
            dma((4, heads)),
            dma((2,)),
            dma((4, heads, steps)),
            dma((4, heads, steps)),
            dma((steps,)),
            dma((steps,)),
            dma((3, heads, steps)),
            dma((3, heads, steps)),
            dma((cp_count - 1,)),
            dma((cp_count - 1,)),
            dma((dp_count - 1,)),
            dma((dp_count - 1,)),
        ],
        compiler_params=pltpu.CompilerParams(
            collective_id=0, has_side_effects=True, vmem_limit_bytes=VMEM_BYTES
        ),
    )(
        queries[0],
        keys[0],
        values[0],
        d_out[0],
        outputs[0],
        log_norm.transpose(2, 0, 1),
        lengths,
        fire_w1,
        fire_b1,
        fire_w2.T,
    )
    return (
        grad_q[None],
        grad_k[None],
        grad_v[None],
        lines[0],
        lines[1],
        second.T,
    )


def on_device(queries, keys, values, outputs, d_out, log_norm, lengths, fire_w1, fire_b1, fire_w2):
    rows_dev = queries.shape[1]
    heads_count = log_norm.shape[2]
    feature_count = queries.shape[2]
    head_size = feature_count // heads_count
    cp_count = lax.axis_size("cp")
    my_index = lax.axis_index("cp")
    length_row = lengths[0]
    reach = GROUP_MOST - 1
    query_heads = queries[0].reshape(rows_dev, heads_count, head_size)
    key_heads = keys[0].reshape(rows_dev, heads_count, head_size)
    value_heads = values[0].reshape(rows_dev, heads_count, head_size)
    grad_heads = d_out[0].reshape(rows_dev, heads_count, head_size)
    out_heads = outputs[0].reshape(rows_dev, heads_count, head_size)
    log_block = log_norm[0]
    delta_block = jnp.einsum(
        "qhd,qhd->qh", grad_heads, out_heads, preferred_element_type=jnp.float32
    )
    token_index = jnp.arange(rows_dev, dtype=jnp.int32)

    def seat_positions(device):
        sequence, offset = seat_of(length_row, device)
        return (sequence, offset * rows_dev + token_index)

    my_seq, my_pos = seat_positions(my_index)
    local = pair_terms(
        query_heads,
        grad_heads,
        log_block,
        delta_block,
        key_heads,
        value_heads,
        my_seq,
        my_pos,
        my_seq,
        my_pos,
        fire_w1,
        fire_b1,
        fire_w2,
    )
    key_value = jnp.stack([key_heads, value_heads])

    def carried_hop(hop_index, carry):
        moving_kv, moving_grads, grad_q, first, bias_sum, second = carry
        moving_kv = rotate_keys(moving_kv)
        moving_grads = shifted_3(moving_grads, "cp", 1)
        key_seq, key_pos = seat_positions((my_index - hop_index) % cp_count)
        terms = pair_terms(
            query_heads,
            grad_heads,
            log_block,
            delta_block,
            moving_kv[0],
            moving_kv[1],
            my_seq,
            my_pos,
            key_seq,
            key_pos,
            fire_w1,
            fire_b1,
            fire_w2,
        )
        moving_grads = moving_grads + jnp.stack([terms[1], terms[2]])
        return (
            moving_kv,
            moving_grads,
            grad_q + terms[0],
            first + terms[3],
            bias_sum + terms[4],
            second + terms[5],
        )

    start = (key_value, jnp.stack([local[1], local[2]]), local[0], local[3], local[4], local[5])
    result = lax.fori_loop(1, GROUP_MOST, carried_hop, start)
    grad_q, first, bias_sum, second = (result[2], result[3], result[4], result[5])
    home_grads = shifted_3(result[1].astype(jnp.bfloat16), "cp", -reach).astype(jnp.float32)
    grad_k, grad_v = (home_grads[0], home_grads[1])
    first, bias_sum, second = lax.psum((first, bias_sum, second), ("cp", "dp"))
    factor = (lax.axis_size("dp") * cp_count * rows_dev) ** (-0.5)
    out_shape = (1, rows_dev, feature_count)
    return (
        grad_q.reshape(out_shape).astype(jnp.bfloat16),
        grad_k.reshape(out_shape).astype(jnp.bfloat16),
        grad_v.reshape(out_shape).astype(jnp.bfloat16),
        first * factor,
        bias_sum * factor,
        second * factor,
    )


def solution(mesh):
    placed = (
        P("dp", "cp", None),
        P("dp", "cp", None),
        P("dp", "cp", None),
        P("dp", "cp", None),
        P("dp", "cp", None),
        P("dp", "cp", None),
        P("dp", None),
        P(),
        P(),
        P(),
    )
    plan = by_heads if mesh.shape["cp"] == 2 * GROUP_MOST else on_device
    return jax.shard_map(
        plan,
        mesh=mesh,
        in_specs=placed,
        out_specs=(P("dp", "cp", None), P("dp", "cp", None), P("dp", "cp", None), P(), P(), P()),
        check_vma=False,
    )
```

```python
import jax
import jax.numpy as jnp
from jax import lax
from jax.experimental import pallas as pl
from jax.experimental.pallas import tpu as pltpu
from jax.sharding import PartitionSpec as P

GROUP_MOST = 4


fire_floor = 64.0


def shifted_2(block, axis, distance):
    devices = range(lax.axis_size(axis))
    route = [(i - distance, i) for i in devices if i - distance in devices]
    return lax.ppermute(block, axis, route)


def shifted_3(shard, axis, by):
    count = lax.axis_size(axis)
    return lax.ppermute(shard, axis, [(i, (i + by) % count) for i in range(count)])


def seat_of(length_row, device):
    ends = jnp.cumsum(length_row)
    sequence = jnp.sum((ends <= device).astype(jnp.int32))
    before = jnp.sum(
        jnp.where(jnp.arange(length_row.shape[0], dtype=jnp.int32) < sequence, length_row, 0)
    )
    return (sequence, device - before)


def pair_terms(
    query_heads,
    grad_heads,
    log_block,
    delta_block,
    key_heads,
    value_heads,
    query_seq,
    query_pos,
    key_seq,
    key_pos,
    fire_w1,
    fire_b1,
    fire_w2,
):
    highest = lax.Precision.HIGHEST
    scale_value = query_heads.shape[2] ** (-0.5)
    allowed = (query_seq == key_seq) & (key_pos[None, :] <= query_pos[:, None])
    distance = jnp.maximum(query_pos[:, None] - key_pos[None, :], 0).astype(jnp.float32)
    denom = jnp.log1p(jnp.maximum(query_pos.astype(jnp.float32), fire_floor))
    ratio = jnp.log1p(distance) / denom[:, None]
    hidden_pre = fire_w1[:, None, None] * ratio[None] + fire_b1[:, None, None]
    hidden_act = jnp.maximum(hidden_pre, 0.0)
    pair_bias = jnp.einsum("cqk,ch->hqk", hidden_act, fire_w2, precision=highest)
    scores = (
        jnp.einsum("qhd,khd->hqk", query_heads, key_heads, preferred_element_type=jnp.float32)
        * scale_value
        + pair_bias
    )
    shifted = jnp.where(allowed[None], scores - log_block.T[:, :, None], -1e30)
    prob_block = jnp.exp(shifted)
    dprob = jnp.einsum("qhd,khd->hqk", grad_heads, value_heads, preferred_element_type=jnp.float32)
    dscore = prob_block * (dprob - delta_block.T[:, :, None])
    prob_low = prob_block.astype(jnp.bfloat16)
    score_low = dscore.astype(jnp.bfloat16)
    grad_query = (
        jnp.einsum("hqk,khd->qhd", score_low, key_heads, preferred_element_type=jnp.float32)
        * scale_value
    )
    grad_key = (
        jnp.einsum("hqk,qhd->khd", score_low, query_heads, preferred_element_type=jnp.float32)
        * scale_value
    )
    grad_value = jnp.einsum(
        "hqk,qhd->khd", prob_low, grad_heads, preferred_element_type=jnp.float32
    )
    grad_second = jnp.einsum("hqk,cqk->ch", dscore, hidden_act, precision=highest)
    grad_act = jnp.einsum("hqk,ch->cqk", dscore, fire_w2, precision=highest)
    grad_pre = jnp.where(hidden_pre > 0, grad_act, 0.0)
    grad_first = jnp.sum(grad_pre * ratio[None], axis=(1, 2))
    grad_bias = jnp.sum(grad_pre, axis=(1, 2))
    return (grad_query, grad_key, grad_value, grad_first, grad_bias, grad_second)


def rotate_keys(key_value):
    return shifted_2(key_value, "cp", 1)


MESH = pl.DeviceIdType.MESH
NT = (((1,), (1,)), ((), ()))
NN = (((1,), (0,)), ((), ()))
TN = (((0,), (0,)), ((), ()))
MASKED = -1e30
VMEM_BYTES = 62 * 2**20
BIAS_ROWS = 32
SUM_ROWS = 64


def exchange_kernel(
    q_ref,
    k_ref,
    v_ref,
    g_ref,
    o_ref,
    log_ref,
    lengths_ref,
    w1_ref,
    b1_ref,
    w2_ref,
    grad_ref,
    second_ref,
    lines_ref,
    held,
    own_g,
    own_o,
    stats,
    pair,
    ratios,
    grads,
    acc,
    coefs,
    cp_slots,
    dp_slots,
    own_sem,
    delta_sem,
    send_in,
    recv_in,
    send_stat,
    recv_stat,
    send_out,
    recv_out,
    send_cp,
    recv_cp,
    send_dp,
    recv_dp,
):
    parts = GROUP_MOST
    heads, tokens, size = held.shape[1:]
    rows = tokens // parts
    hidden = w1_ref.shape[0]
    heads_count = heads * parts
    delta_at = stats.shape[1] // 2
    cp_count, dp_count = cp_slots.shape[0], dp_slots.shape[0]
    scale_value = size ** (-0.5)
    me = lax.axis_index("cp")
    my_dp = lax.axis_index("dp")
    rank = lax.rem(me, parts)
    base = me - rank
    inputs = (q_ref, k_ref, v_ref, g_ref)
    results = tuple(grad_ref.at[array] for array in range(3))

    def dot(a, b, dims):
        return lax.dot_general(a, b, dims, preferred_element_type=jnp.float32)

    def peer_of(step):
        return lax.rem(rank + step, parts)

    def row_block(index):
        return pl.ds(pl.multiple_of(index * rows, rows), rows)

    def head_columns(part, head):
        return pl.ds(pl.multiple_of((part * heads + head) * size, size), size)

    def stat_copy(step):
        return pltpu.make_async_remote_copy(
            src_ref=stats.at[rank],
            dst_ref=stats.at[rank],
            send_sem=send_stat.at[step - 1],
            recv_sem=recv_stat.at[step - 1],
            device_id={"cp": base + peer_of(step)},
            device_id_type=MESH,
        )

    def in_copy(array, head, step):
        peer = peer_of(step)
        return pltpu.make_async_remote_copy(
            src_ref=inputs[array].at[:, head_columns(peer, head)],
            dst_ref=held.at[array, head, row_block(rank), :],
            send_sem=send_in.at[array, head, step - 1],
            recv_sem=recv_in.at[array, head, step - 1],
            device_id={"cp": base + peer},
            device_id_type=MESH,
        )

    def own_copy(array, head):
        return pltpu.make_async_copy(
            inputs[array].at[:, head_columns(rank, head)],
            held.at[array, head, row_block(rank), :],
            own_sem.at[array, head],
        )

    def out_copy(array, head, step):
        peer = peer_of(step)
        return pltpu.make_async_remote_copy(
            src_ref=grads.at[array, head, row_block(peer), :],
            dst_ref=results[array].at[:, head_columns(rank, head)],
            send_sem=send_out.at[array, head, step - 1],
            recv_sem=recv_out.at[array, head, step - 1],
            device_id={"cp": base + peer},
            device_id_type=MESH,
        )

    def cp_copy(step):
        return pltpu.make_async_remote_copy(
            src_ref=cp_slots.at[me],
            dst_ref=cp_slots.at[me],
            send_sem=send_cp.at[step - 1],
            recv_sem=recv_cp.at[step - 1],
            device_id={"cp": lax.rem(me + step, cp_count)},
            device_id_type=MESH,
        )

    def dp_copy(step):
        return pltpu.make_async_remote_copy(
            src_ref=dp_slots.at[my_dp],
            dst_ref=dp_slots.at[my_dp],
            send_sem=send_dp.at[step - 1],
            recv_sem=recv_dp.at[step - 1],
            device_id={"dp": lax.rem(my_dp + step, dp_count)},
            device_id_type=MESH,
        )

    delta_copies = (
        pltpu.make_async_copy(g_ref, own_g, delta_sem.at[0]),
        pltpu.make_async_copy(o_ref, own_o, delta_sem.at[1]),
    )
    for copy in delta_copies:
        copy.start()

    barrier = pltpu.get_barrier_semaphore()
    for step in range(1, cp_count):
        pl.semaphore_signal(
            barrier, inc=1, device_id={"cp": lax.rem(me + step, cp_count)}, device_id_type=MESH
        )
    for step in range(1, dp_count):
        pl.semaphore_signal(
            barrier, inc=1, device_id={"dp": lax.rem(my_dp + step, dp_count)}, device_id_type=MESH
        )
    pl.semaphore_wait(barrier, cp_count + dp_count - 2)

    def send_head(head, carry):
        for step in (2, 1, 3):
            for array in range(4):
                in_copy(array, head, step).start()
        for array in range(4):
            own_copy(array, head).start()
        return carry

    early = 2
    lax.fori_loop(0, early, send_head, 0)

    stats[rank] = jnp.zeros(stats.shape[1:], jnp.float32)
    stats[rank, 0:heads_count, :] = log_ref[:, 0, :]
    for copy in delta_copies:
        copy.wait()
    ones = jnp.ones((8, 2 * size), jnp.bfloat16)

    def delta_head(head, carry):
        columns = pl.ds(pl.multiple_of(head * size, size), size)
        product = own_g[:, columns].astype(jnp.float32) * own_o[:, columns].astype(jnp.float32)
        high = product.astype(jnp.bfloat16)
        rest = (product - high.astype(jnp.float32)).astype(jnp.bfloat16)
        row = dot(ones, jnp.concatenate([high, rest], axis=1), NT)
        stats[rank, pl.ds(delta_at + head, 1), :] = row[0:1]
        return carry

    lax.fori_loop(0, heads_count, delta_head, 0)
    for step in range(1, parts):
        stat_copy(step).start()
    lax.fori_loop(early, heads, send_head, 0)

    def bias_column(block, carry):
        columns = row_block(block)
        start = jnp.int32(0)
        end = jnp.int32(0)
        for index in range(lengths_ref.shape[1]):
            start = jnp.where(end <= base + block, end, start)
            end = end + lengths_ref[0, index]
        start = (start - base) * rows
        query_row = block * rows + lax.broadcasted_iota(jnp.int32, (1, rows), 1)
        position = (query_row - start).astype(jnp.float32)
        rden = 1.0 / jnp.log(1.0 + jnp.maximum(position, fire_floor))

        def bias_rows(chunk, carry):
            at = pl.ds(pl.multiple_of(chunk * BIAS_ROWS, BIAS_ROWS), BIAS_ROWS)
            key_at = chunk * BIAS_ROWS + lax.broadcasted_iota(jnp.int32, (BIAS_ROWS, rows), 0)
            query_at = block * rows + lax.broadcasted_iota(jnp.int32, (BIAS_ROWS, rows), 1)
            allowed = (key_at >= start) & (key_at <= query_at)
            distance = jnp.maximum(query_at - key_at, 0).astype(jnp.float32)
            ratio = jnp.log(1.0 + distance) * rden
            ratios[at, columns] = ratio
            totals = [jnp.zeros((BIAS_ROWS, rows), jnp.float32) for _ in range(heads)]
            for unit in range(hidden):
                act = jnp.maximum(ratio * w1_ref[unit] + b1_ref[unit], 0.0)
                for head in range(heads):
                    totals[head] = totals[head] + act * w2_ref[rank * heads + head, unit]
            for head in range(heads):
                pair[head, at, columns] = jnp.where(allowed, totals[head], MASKED)
            return carry

        return lax.fori_loop(0, (block + 1) * (rows // BIAS_ROWS), bias_rows, carry)

    lax.fori_loop(0, parts, bias_column, 0)
    half = 2 * rows
    for head in range(heads):
        for first in range(0, parts, 2):
            pair[head, (first + 1) * rows : (first + 2) * rows, first * rows : (first + 1) * rows] = (
                jnp.full((rows, rows), MASKED, jnp.float32)
            )
    acc[...] = jnp.zeros_like(acc)
    unit_at = lax.broadcasted_iota(jnp.int32, (hidden, 128), 0)
    lane_at = lax.broadcasted_iota(jnp.int32, (hidden, 128), 1)
    coef = jnp.zeros((hidden, 128), jnp.float32)
    for unit in range(hidden):
        line = jnp.where(lane_at == 0, w1_ref[unit], b1_ref[unit])
        for head in range(heads):
            line = jnp.where(lane_at == 2 + head, w2_ref[rank * heads + head, unit], line)
        coef = jnp.where(unit_at == unit, line, coef)
    coefs[...] = coef

    for step in range(1, parts):
        stat_copy(step).wait_recv()

    def one_head(head, carry):
        for array in range(4):
            own_copy(array, head).wait()
        for step in (2, 1, 3):
            for array in range(4):
                in_copy(array, head, step).wait_recv()
        at = rank * heads + head
        log_row = jnp.concatenate([stats[part, pl.ds(at, 1), :] for part in range(parts)], axis=1)
        delta_row = jnp.concatenate(
            [stats[part, pl.ds(delta_at + at, 1), :] for part in range(parts)], axis=1
        )

        dq = [None, None]
        dk = [None, None]
        dv = [None, None]

        def plus(total, term):
            return term if total is None else total + term

        for kt, qt in ((0, 0), (0, 1), (1, 1)):
            krows = slice(kt * half, (kt + 1) * half)
            qrows = slice(qt * half, (qt + 1) * half)
            q = held[0, head, qrows, :]
            k = held[1, head, krows, :]
            v = held[2, head, krows, :]
            g = held[3, head, qrows, :]
            scores = dot(k, q, NT) * scale_value + pair[head, krows, qrows]
            prob = jnp.exp(scores - log_row[:, qrows])
            dscore = prob * (dot(v, g, NT) - delta_row[:, qrows])
            pair[head, krows, qrows] = dscore
            prob_low = prob.astype(jnp.bfloat16)
            score_low = dscore.astype(jnp.bfloat16)
            dv[kt] = plus(dv[kt], dot(prob_low, g, NN))
            dk[kt] = plus(dk[kt], dot(score_low, q, NN))
            dq[qt] = plus(dq[qt], dot(score_low, k, TN))
        for tile in range(2):
            trows = slice(tile * half, (tile + 1) * half)
            grads[0, head, trows, :] = (dq[tile] * scale_value).astype(jnp.bfloat16)
            grads[1, head, trows, :] = (dk[tile] * scale_value).astype(jnp.bfloat16)
            grads[2, head, trows, :] = dv[tile].astype(jnp.bfloat16)
        for array in range(3):
            results[array][:, head_columns(rank, head)] = grads[array, head, row_block(rank), :]
        return carry

    def return_head(head, carry):
        for step in (2, 1, 3):
            for array in range(3):
                out_copy(array, head, step).start()
        return carry

    prompt = heads - 2
    lax.fori_loop(0, prompt, lambda head, carry: return_head(head, one_head(head, carry)), 0)
    lax.fori_loop(prompt, heads, one_head, 0)

    def sum_column(block, carry):
        columns = row_block(block)

        def sum_rows(chunk, carry):
            at = pl.ds(pl.multiple_of(chunk * SUM_ROWS, SUM_ROWS), SUM_ROWS)
            ratio = ratios[at, columns]
            flat = [pair[head, at, columns] for head in range(heads)]
            lives, terms = [], []
            for row in range(0, SUM_ROWS, 8):
                part = ratio[row : row + 8]
                live = [
                    jnp.where(part * w1_ref[unit] > -b1_ref[unit], 1.0, 0.0)
                    for unit in range(hidden)
                ]
                lives.append(jnp.concatenate(live, axis=0).astype(jnp.bfloat16))
                term = [flat[head][row : row + 8] for head in range(heads)]
                term = jnp.concatenate(term + [one * part for one in term], axis=0)
                high = term.astype(jnp.bfloat16)
                rest = (term - high.astype(jnp.float32)).astype(jnp.bfloat16)
                terms.append(jnp.concatenate([high, rest], axis=0))
            acc[...] += dot(
                jnp.concatenate(lives, axis=1), jnp.concatenate(terms, axis=1), NT
            )
            return carry

        return lax.fori_loop(0, (block + 1) * (rows // SUM_ROWS), sum_rows, carry)

    lax.fori_loop(0, parts, sum_column, 0)

    across = acc.shape[1]
    same = lax.rem(lax.broadcasted_iota(jnp.int32, acc.shape, 0), 8) == lax.rem(
        lax.broadcasted_iota(jnp.int32, acc.shape, 1), 8
    )
    folded = jnp.sum(jnp.where(same, acc[...], 0.0).reshape(hidden, 8, across), axis=1)
    kind = lax.rem(lax.broadcasted_iota(jnp.int32, (hidden, across), 1) // 8, 2 * heads)
    lane = lax.broadcasted_iota(jnp.int32, (hidden, 128), 1)
    message = jnp.zeros((hidden, 128), jnp.float32)
    first = jnp.zeros((hidden, 1), jnp.float32)
    bias_sum = jnp.zeros((hidden, 1), jnp.float32)
    w1_column, b1_column = coefs[:, 0:1], coefs[:, 1:2]
    for head in range(heads):
        flat = jnp.sum(jnp.where(kind == head, folded, 0.0), axis=1, keepdims=True)
        tilted = jnp.sum(jnp.where(kind == heads + head, folded, 0.0), axis=1, keepdims=True)
        weight = coefs[:, 2 + head : 3 + head]
        first = first + tilted * weight
        bias_sum = bias_sum + flat * weight
        second = tilted * w1_column + flat * b1_column
        message = jnp.where(lane == rank * heads + head, second, message)
    message = jnp.where(lane == heads_count, first, message)
    message = jnp.where(lane == heads_count + 1, bias_sum, message)
    cp_slots[me] = message
    for step in range(1, cp_count):
        cp_copy(step).start()
    lax.fori_loop(prompt, heads, return_head, 0)
    for step in range(1, cp_count):
        cp_copy(step).wait()
    total = cp_slots[0]
    for index in range(1, cp_count):
        total = total + cp_slots[index]
    dp_slots[my_dp] = total
    for step in range(1, dp_count):
        dp_copy(step).start()
    for step in range(1, dp_count):
        dp_copy(step).wait()
    total = dp_slots[0]
    for index in range(1, dp_count):
        total = total + dp_slots[index]
    total = (total * (dp_count * cp_count * rows) ** (-0.5)).T
    second_ref[...] = total[0:heads_count]
    lines_ref[...] = total[heads_count : heads_count + 2]

    def drain_head(head, carry):
        for step in (2, 1, 3):
            for array in range(4):
                in_copy(array, head, step).wait_send()
            for array in range(3):
                out_copy(array, head, step).wait()
        return carry

    lax.fori_loop(0, heads, drain_head, 0)
    for step in range(1, parts):
        stat_copy(step).wait_send()


def by_heads(queries, keys, values, outputs, d_out, log_norm, lengths, fire_w1, fire_b1, fire_w2):
    rows_dev = queries.shape[1]
    heads_count = log_norm.shape[2]
    feature_count = queries.shape[2]
    head_size = feature_count // heads_count
    cp_count, dp_count = lax.axis_size("cp"), lax.axis_size("dp")
    parts = GROUP_MOST
    heads = heads_count // parts
    hidden = fire_w1.shape[0]
    tokens = parts * rows_dev
    stat_rows = 2 * (-(-heads_count // 8) * 8)

    hbm = pl.BlockSpec(memory_space=pltpu.HBM)
    vmem = pl.BlockSpec(memory_space=pltpu.VMEM)
    smem = pl.BlockSpec(memory_space=pltpu.SMEM)
    low = jnp.bfloat16
    wide = jnp.float32
    block = jax.ShapeDtypeStruct((3, rows_dev, feature_count), low)
    steps = parts - 1
    dma = pltpu.SemaphoreType.DMA
    joined, second, lines = pl.pallas_call(
        exchange_kernel,
        out_shape=(
            block,
            jax.ShapeDtypeStruct((heads_count, hidden), wide),
            jax.ShapeDtypeStruct((2, hidden), wide),
        ),
        in_specs=[hbm] * 5 + [vmem] + [smem] * 4,
        out_specs=(vmem,) * 3,
        scratch_shapes=[
            pltpu.VMEM((4, heads, tokens, head_size), low),
            pltpu.VMEM((rows_dev, feature_count), low),
            pltpu.VMEM((rows_dev, feature_count), low),
            pltpu.VMEM((parts, stat_rows, rows_dev), wide),
            pltpu.VMEM((heads, tokens, tokens), wide),
            pltpu.VMEM((tokens, tokens), wide),
            pltpu.VMEM((3, heads, tokens, head_size), low),
            pltpu.VMEM((hidden * 8, 4 * heads * 8), wide),
            pltpu.VMEM((hidden, 128), wide),
            pltpu.VMEM((cp_count, hidden, 128), wide),
            pltpu.VMEM((dp_count, hidden, 128), wide),
            dma((4, heads)),
            dma((2,)),
            dma((4, heads, steps)),
            dma((4, heads, steps)),
            dma((steps,)),
            dma((steps,)),
            dma((3, heads, steps)),
            dma((3, heads, steps)),
            dma((cp_count - 1,)),
            dma((cp_count - 1,)),
            dma((dp_count - 1,)),
            dma((dp_count - 1,)),
        ],
        compiler_params=pltpu.CompilerParams(
            collective_id=0, has_side_effects=True, vmem_limit_bytes=VMEM_BYTES
        ),
    )(
        queries[0],
        keys[0],
        values[0],
        d_out[0],
        outputs[0],
        log_norm.transpose(2, 0, 1),
        lengths,
        fire_w1,
        fire_b1,
        fire_w2.T,
    )
    return (
        joined[0:1],
        joined[1:2],
        joined[2:3],
        lines[0],
        lines[1],
        second.T,
    )


def on_device(queries, keys, values, outputs, d_out, log_norm, lengths, fire_w1, fire_b1, fire_w2):
    rows_dev = queries.shape[1]
    heads_count = log_norm.shape[2]
    feature_count = queries.shape[2]
    head_size = feature_count // heads_count
    cp_count = lax.axis_size("cp")
    my_index = lax.axis_index("cp")
    length_row = lengths[0]
    reach = GROUP_MOST - 1
    query_heads = queries[0].reshape(rows_dev, heads_count, head_size)
    key_heads = keys[0].reshape(rows_dev, heads_count, head_size)
    value_heads = values[0].reshape(rows_dev, heads_count, head_size)
    grad_heads = d_out[0].reshape(rows_dev, heads_count, head_size)
    out_heads = outputs[0].reshape(rows_dev, heads_count, head_size)
    log_block = log_norm[0]
    delta_block = jnp.einsum(
        "qhd,qhd->qh", grad_heads, out_heads, preferred_element_type=jnp.float32
    )
    token_index = jnp.arange(rows_dev, dtype=jnp.int32)

    def seat_positions(device):
        sequence, offset = seat_of(length_row, device)
        return (sequence, offset * rows_dev + token_index)

    my_seq, my_pos = seat_positions(my_index)
    local = pair_terms(
        query_heads,
        grad_heads,
        log_block,
        delta_block,
        key_heads,
        value_heads,
        my_seq,
        my_pos,
        my_seq,
        my_pos,
        fire_w1,
        fire_b1,
        fire_w2,
    )
    key_value = jnp.stack([key_heads, value_heads])

    def carried_hop(hop_index, carry):
        moving_kv, moving_grads, grad_q, first, bias_sum, second = carry
        moving_kv = rotate_keys(moving_kv)
        moving_grads = shifted_3(moving_grads, "cp", 1)
        key_seq, key_pos = seat_positions((my_index - hop_index) % cp_count)
        terms = pair_terms(
            query_heads,
            grad_heads,
            log_block,
            delta_block,
            moving_kv[0],
            moving_kv[1],
            my_seq,
            my_pos,
            key_seq,
            key_pos,
            fire_w1,
            fire_b1,
            fire_w2,
        )
        moving_grads = moving_grads + jnp.stack([terms[1], terms[2]])
        return (
            moving_kv,
            moving_grads,
            grad_q + terms[0],
            first + terms[3],
            bias_sum + terms[4],
            second + terms[5],
        )

    start = (key_value, jnp.stack([local[1], local[2]]), local[0], local[3], local[4], local[5])
    result = lax.fori_loop(1, GROUP_MOST, carried_hop, start)
    grad_q, first, bias_sum, second = (result[2], result[3], result[4], result[5])
    home_grads = shifted_3(result[1].astype(jnp.bfloat16), "cp", -reach).astype(jnp.float32)
    grad_k, grad_v = (home_grads[0], home_grads[1])
    first, bias_sum, second = lax.psum((first, bias_sum, second), ("cp", "dp"))
    factor = (lax.axis_size("dp") * cp_count * rows_dev) ** (-0.5)
    out_shape = (1, rows_dev, feature_count)
    return (
        grad_q.reshape(out_shape).astype(jnp.bfloat16),
        grad_k.reshape(out_shape).astype(jnp.bfloat16),
        grad_v.reshape(out_shape).astype(jnp.bfloat16),
        first * factor,
        bias_sum * factor,
        second * factor,
    )


def solution(mesh):
    placed = (
        P("dp", "cp", None),
        P("dp", "cp", None),
        P("dp", "cp", None),
        P("dp", "cp", None),
        P("dp", "cp", None),
        P("dp", "cp", None),
        P("dp", None),
        P(),
        P(),
        P(),
    )
    plan = by_heads if mesh.shape["cp"] == 2 * GROUP_MOST else on_device
    return jax.shard_map(
        plan,
        mesh=mesh,
        in_specs=placed,
        out_specs=(P("dp", "cp", None), P("dp", "cp", None), P("dp", "cp", None), P(), P(), P()),
        check_vma=False,
    )
```
